128 devices in a mesh: compute: 8 (over z_lo, x), memory: 8 (over y, core), pair: 2 (over z_hi).
Axes of the slice: x: 4, y: 4, z: 4 (z_hi: 2, z_lo: 2; z = z_hi * 2 + z_lo), core: 2. Of those that a mesh axis runs over, the one named last changes fastest.
Arguments:
- hidden: bfloat16 [2048, 8192], P('memory', 'pair'), may hold values from -80 to 80
- norm_gain: bfloat16 [8192], P('pair'), may hold values from 0.25 to 1.75
- w_query: bfloat16 [8192, 8192], P('pair', 'compute'), may hold values from -0.0625 to 0.0625
- w_key: bfloat16 [8192, 1024], P('pair', 'compute'), may hold values from -0.0625 to 0.0625
- w_value: bfloat16 [8192, 1024], P('pair', 'compute'), may hold values from -0.0625 to 0.0625
- query_bias: bfloat16 [8192], P('compute'), may hold values from -4 to 4
- key_bias: bfloat16 [1024], P('compute'), may hold values from -4 to 4
- value_bias: bfloat16 [1024], P('compute'), may hold values from -4 to 4
- prefix_keys: bfloat16 [8, 8192, 1024], P('memory', 'pair', 'compute'), may hold values from -240 to 240
- prefix_values: bfloat16 [8, 8192, 1024], P('memory', 'pair', 'compute'), may hold values from -12 to 12
- reply_keys: bfloat16 [8, 384, 128, 1024], P('memory', 'pair', None, 'compute'), may hold values from -9 to 9
- reply_values: bfloat16 [8, 384, 128, 1024], P('memory', 'pair', None, 'compute'), may hold values from -12 to 12
- reply_length: int32 [2048], P(('memory', 'pair')), may hold values from 1 to 128
- prefix_ids: int32 [2048], P(('memory', 'pair')), may hold values from 0 to 7, as said below
- prompt_home: int32 [8], replicated, may hold values from 0 to 7, as said below
Outputs:
- attention: bfloat16 [2048, 8192], P(('memory', 'pair'), 'compute')
- stored_rows: bfloat16 [2, 8, 384, 1024], P(None, 'memory', None, 'compute')
The draws below stay inside these ranges and needn't reach their ends.
Inputs may be any that keep to these rules, and one draw needn't show every extreme that they name: `prefix_ids`: among the 128 rollouts of each aligned block (the rollouts of one device, blocks in the order of memory then pair), at most 24 have a prompt whose prompt_home // 1 is the same memory index; in every draw one memory index gets exactly 24 from every block. `prompt_home`: A permutation of the prompts.
All inputs are finite; a program needn't handle non-finite values.
Results may differ from the reference program's by a relative error of at most 0.012.
The reference program's roundings to bfloat16 on the way (of `normed`, `queries` and `rounded`) count: a program that leaves them out, or rounds other values in their place, can miss the bound.
Values may be sent and summed in bfloat16 or wider, within the bound.
No kernel may reach another device: no remote copies, remote signals or barrier semaphores. Data moves between devices by JAX's collectives and lax.ppermute only.
A program may use at most 192 MiB of HBM per device.

```python
import math
import jax
import jax.numpy as jnp
from jax import lax

D = 8192
H = 64
KVH = 8
HD = 128
ROLL_DEV = 128
PREFIX = 8192
RMAX = 128
PROMPT_HOLD = 1
B = 2048
HOLDERS = 8
CAP = 24
SLOTS = 384
PROMPTS = 8


def route_tables(key):
    busy_key, block_key, prompt_key, home_key = jax.random.split(key, 4)
    block_total = B // ROLL_DEV
    busiest = jax.random.randint(busy_key, (), 0, HOLDERS)

    def one_block(block_seed):
        order_key, spread_key = jax.random.split(block_seed)
        places = jax.random.permutation(order_key, HOLDERS * CAP)
        others = (places // CAP != busiest).astype(jnp.int32)
        ranked = places[jnp.argsort(others, stable=True)]
        chosen = jax.random.permutation(spread_key, ranked[:ROLL_DEV])
        return chosen // CAP
    owners = jax.vmap(one_block)(jax.random.split(block_key, block_total)).reshape(B)
    within = jax.random.randint(prompt_key, (B,), 0, PROMPT_HOLD)
    prompt_homes = jax.random.permutation(home_key, PROMPTS).astype(jnp.int32)
    inverse = jnp.argsort(prompt_homes).astype(jnp.int32)
    return (prompt_homes, inverse[owners * PROMPT_HOLD + within])


def draw_prefix_ids(key, part):
    return route_tables(key)[1].astype(jnp.int32)


def draw_prompt_home(key, part):
    return route_tables(key)[0].astype(jnp.int32)


def draw_reply_length(key, part):
    key = jax.random.fold_in(key, 7)
    length_key, spot_key = jax.random.split(key)
    lengths = jax.random.randint(length_key, (B,), 1, RMAX + 1)
    longest = jax.random.randint(spot_key, (), 0, B)
    return jnp.where(jnp.arange(B) == longest, RMAX, lengths).astype(jnp.int32)


def draw_hidden(key, part):
    key = jax.random.fold_in(key, 3)
    entry_key, row_key = jax.random.split(key, 2)
    column_scale = 1.0 + 2.0 * jnp.arange(D, dtype=jnp.float32) / D
    row_scale = jnp.exp(jax.random.uniform(row_key, (B, 1), jnp.float32, math.log(0.5), math.log(5.0)))
    entries = jnp.clip(jax.random.normal(entry_key, (B, D), jnp.float32), -5.0, 5.0)
    return (entries * row_scale * column_scale[None, :]).astype(jnp.bfloat16)


def draw_prefix_keys(key, part):
    key = jax.random.fold_in(key, 5)
    entry_key = jax.random.fold_in(key, 0)
    full_shape = (PROMPTS, PREFIX, KVH * HD)
    return jnp.clip(jax.random.normal(entry_key, full_shape, jnp.float32) * 1.5, -9.0, 9.0).astype(jnp.bfloat16)


def steps_of(stream_key, shape, cuts, smallest, largest):
    def one(dim, shards_of):
        heights = jax.random.uniform(jax.random.fold_in(jax.random.fold_in(stream_key, 6), dim), (shards_of,), jnp.float32, smallest / len(cuts), largest / len(cuts))
        return jnp.repeat(jnp.exp(heights), shape[dim] // shards_of).reshape((-1,) + (1,) * (len(shape) - dim - 1))

    loudness = one(*cuts[0])
    for cut in cuts[1:]:
        loudness = loudness * one(*cut)
    return loudness


def normal_values(rng, shape, scale, bound, cuts=(), kind=jnp.bfloat16):
    result = scale * jax.random.normal(rng, shape, jnp.float32)
    if cuts:
        result = result * steps_of(rng, shape, cuts, -0.22, 0.18)
    return jnp.clip(result, -bound, bound).astype(kind)


def setup_inputs(seed: int = 0) -> dict:
    arg_keys = jax.random.split(jax.random.key(seed), 16)
    hidden = draw_hidden(jax.random.fold_in(arg_keys[15], 71), 0)
    norm_gain = jnp.clip(1.0 + 0.15 * jax.random.normal(arg_keys[1], (D,), jnp.float32), 0.25, 1.75).astype(jnp.bfloat16)
    w_query = normal_values(arg_keys[2], (D, H * HD), D ** -0.5, 0.0625, ((0, 2), (1, 8)))
    w_key = normal_values(arg_keys[3], (D, KVH * HD), D ** -0.5, 0.0625, ((0, 2), (1, 8)))
    w_value = normal_values(arg_keys[4], (D, KVH * HD), D ** -0.5, 0.0625, ((0, 2), (1, 8)))
    query_bias = normal_values(arg_keys[5], (H * HD,), 1.0, 4.0, ((0, 8),))
    key_bias = normal_values(arg_keys[6], (KVH * HD,), 1.0, 4.0, ((0, 8),))
    value_bias = normal_values(arg_keys[7], (KVH * HD,), 1.0, 4.0, ((0, 8),))
    prefix_keys = draw_prefix_keys(jax.random.fold_in(arg_keys[15], 71), 0)
    prefix_values = normal_values(arg_keys[9], (PROMPTS, PREFIX, KVH * HD), 2.0, 12.0, ((0, 8), (1, 2), (2, 8)))
    reply_keys = normal_values(arg_keys[10], (HOLDERS, SLOTS, RMAX, KVH * HD), 1.5, 9.0, ((0, 8), (1, 2), (3, 8)))
    reply_values = normal_values(arg_keys[11], (HOLDERS, SLOTS, RMAX, KVH * HD), 2.0, 12.0, ((0, 8), (1, 2), (3, 8)))
    reply_length = draw_reply_length(jax.random.fold_in(arg_keys[15], 71), 0)
    prefix_ids = draw_prefix_ids(jax.random.fold_in(arg_keys[15], 71), 0)
    prompt_home = draw_prompt_home(jax.random.fold_in(arg_keys[15], 71), 0)
    return {"hidden": hidden, "norm_gain": norm_gain, "w_query": w_query, "w_key": w_key, "w_value": w_value, "query_bias": query_bias, "key_bias": key_bias, "value_bias": value_bias, "prefix_keys": prefix_keys, "prefix_values": prefix_values, "reply_keys": reply_keys, "reply_values": reply_values, "reply_length": reply_length, "prefix_ids": prefix_ids, "prompt_home": prompt_home}


EPSILON = 1e-06
ROPE_BASE = 1000000.0
MASKED = -1e+30

def rotate(vectors, position):
    half_dim = vectors.shape[-1] // 2
    ladder = jnp.arange(half_dim, dtype=jnp.float32) * (2.0 / vectors.shape[-1])
    frequency = jnp.power(ROPE_BASE, -ladder)
    angles = position.astype(jnp.float32)[:, None, None] * frequency
    cosine = jnp.cos(angles)
    sine_part = jnp.sin(angles)
    first_half = vectors[..., :half_dim]
    second_half = vectors[..., half_dim:]
    return jnp.concatenate([first_half * cosine - second_half * sine_part, second_half * cosine + first_half * sine_part], axis=-1)

def attend_one(query_row, fresh_key, fresh_value, prompt_slot, owner_index, slot_index, length, prefix_keys, prefix_values, reply_keys, reply_values):
    key_rows = jnp.concatenate([prefix_keys[prompt_slot], reply_keys[owner_index, slot_index], fresh_key[None, :]], axis=0)
    value_rows = jnp.concatenate([prefix_values[prompt_slot], reply_values[owner_index, slot_index], fresh_value[None, :]], axis=0)
    key_rows = key_rows.astype(jnp.float32).reshape(-1, KVH, HD)
    value_rows = value_rows.astype(jnp.float32).reshape(-1, KVH, HD)
    visible = jnp.concatenate([jnp.ones((PREFIX,), jnp.bool_), jnp.arange(RMAX, dtype=jnp.int32) < length, jnp.ones((1,), jnp.bool_)])
    queries = query_row.astype(jnp.float32).reshape(KVH, H // KVH, HD)
    scores = jnp.einsum('kgd,tkd->kgt', queries, key_rows) * HD ** (-0.5)
    scores = jnp.where(visible, scores, MASKED)
    highest = lax.optimization_barrier(jnp.max(scores, axis=-1, keepdims=True))
    weights = jnp.where(visible, jnp.exp(scores - highest), 0.0)
    rounded = lax.optimization_barrier(weights.astype(jnp.bfloat16)).astype(jnp.float32)
    mixed = jnp.einsum('kgt,tkd->kgd', rounded, value_rows) / lax.optimization_barrier(jnp.sum(weights, axis=-1))[..., None]
    return mixed.reshape(H * HD)

def reference(hidden, norm_gain, w_query, w_key, w_value, query_bias, key_bias, value_bias, prefix_keys, prefix_values, reply_keys, reply_values, reply_length, prefix_ids, prompt_home):
    widened = hidden.astype(jnp.float32)
    squares = lax.optimization_barrier(jnp.mean(widened * widened, axis=1, keepdims=True))
    normed = (widened * lax.rsqrt(squares + EPSILON) * norm_gain.astype(jnp.float32)).astype(jnp.bfloat16)
    query_part = jnp.dot(normed, w_query, preferred_element_type=jnp.float32) + query_bias.astype(jnp.float32)
    key_part = jnp.dot(normed, w_key, preferred_element_type=jnp.float32) + key_bias.astype(jnp.float32)
    value_part = jnp.dot(normed, w_value, preferred_element_type=jnp.float32) + value_bias.astype(jnp.float32)
    position = PREFIX + reply_length
    queries = rotate(query_part.reshape(B, H, HD), position).reshape(B, H * HD).astype(jnp.bfloat16)
    fresh_keys = rotate(key_part.reshape(B, KVH, HD), position).reshape(B, KVH * HD).astype(jnp.bfloat16)
    fresh_values = value_part.astype(jnp.bfloat16)
    places = prompt_home[prefix_ids].astype(jnp.int32)
    owners = places // PROMPT_HOLD
    owner_table = (owners[:, None] == jnp.arange(HOLDERS, dtype=jnp.int32)[None, :]).astype(jnp.int32)
    owner_table = owner_table.reshape(B // ROLL_DEV, ROLL_DEV, HOLDERS)
    earlier = jnp.cumsum(owner_table, axis=1) - owner_table
    ranks = lax.optimization_barrier(jnp.sum(earlier * owner_table, axis=2)).reshape(B)
    slots = jnp.arange(B, dtype=jnp.int32) // ROLL_DEV * CAP + ranks
    stored_rows = jnp.zeros((2, HOLDERS, SLOTS, KVH * HD), jnp.bfloat16)
    stored_rows = stored_rows.at[0, owners, slots].set(fresh_keys)
    stored_rows = stored_rows.at[1, owners, slots].set(fresh_values)

    def attend_rollout(query_row, key_row, value_row, prompt_slot, owner_index, slot_index, length):
        return attend_one(query_row, key_row, value_row, prompt_slot, owner_index, slot_index, length, prefix_keys, prefix_values, reply_keys, reply_values)

    def attend_group(group_items):
        return jax.vmap(attend_rollout)(*group_items)
    group_items = tuple((member.reshape((B // 8, 8) + member.shape[1:]) for member in (queries, fresh_keys, fresh_values, places, owners, slots, reply_length)))
    mixed = lax.map(attend_group, group_items)
    attention = mixed.reshape(B, H * HD).astype(jnp.bfloat16)
    return (attention, stored_rows)
```

```python
from functools import partial

import jax
import jax.numpy as jnp
from jax import lax
from jax.experimental import pallas as pl
from jax.experimental.pallas import tpu as pltpu
from jax.sharding import PartitionSpec as P

D = 8192
HD = 128
PREFIX = 8192
EPSILON = 1e-06
ROPE_BASE = 1000000.0
MASKED = -1e30
ROWS = 128
HOLDERS = 8
CAP = 24
HEADS = 8
QW = HEADS * HD
SLOTS = HOLDERS * CAP
LENGTH_AT = QW
KEY_AT = QW + HD
VALUE_AT = QW + 2 * HD
ROW_WIDTH = QW + 3 * HD
SCALE = 1.4426950408889634 / HD**0.5
F32 = jnp.float32
BF16 = jnp.bfloat16
VMEM_LIMIT = 56 * 1024 * 1024


def params(**more):
    return pltpu.CompilerParams(vmem_limit_bytes=VMEM_LIMIT, **more)


def lane_ids(shape):
    return lax.broadcasted_iota(jnp.int32, shape, len(shape) - 1)


def to_column(row):
    size = row.shape[1]
    spread = jnp.broadcast_to(row, (size, size))
    diagonal = lax.broadcasted_iota(jnp.int32, (size, size), 0) == lane_ids((size, size))
    return jnp.sum(jnp.where(diagonal, spread, jnp.zeros_like(spread)), axis=1, keepdims=True)


def project_kernel(
    span_ref, inverse_ref, hidden_ref, gain_ref, wq_ref, wk_ref, wv_ref, keep_ref, send_ref, scale_ref
):
    span = span_ref[0]
    step = pl.program_id(0)

    @pl.when(step == 0)
    def _():
        first = to_column(inverse_ref[0:1, :])
        second = to_column(inverse_ref[1:2, :])
        scale_ref[0:ROWS, :] = jnp.broadcast_to(jnp.where(span == 0, first, second), (ROWS, HD))
        scale_ref[ROWS:, :] = jnp.broadcast_to(jnp.where(span == 0, second, first), (ROWS, HD))
        keep_ref[...] = jnp.zeros_like(keep_ref)
        send_ref[...] = jnp.zeros_like(send_ref)

    own_start = pl.multiple_of(span * ROWS, ROWS)
    other_start = pl.multiple_of((1 - span) * ROWS, ROWS)
    gain = gain_ref[...].astype(F32)
    for start, where, out_ref in ((other_start, ROWS, send_ref), (own_start, 0, keep_ref)):
        rows = hidden_ref[pl.ds(start, ROWS), :].astype(F32)
        normed = (rows * scale_ref[where : where + ROWS, 0:1] * gain).astype(BF16)
        for at, w_ref in ((0, wq_ref), (QW, wk_ref), (QW + HD, wv_ref)):
            width = w_ref.shape[1]
            out_ref[:, at : at + width] += jnp.dot(normed, w_ref[...], preferred_element_type=F32)


def project(span, inverse, hidden, gain, w_query, w_key, w_value):
    depth = hidden.shape[1]
    part = 1024
    width = QW + 2 * HD
    out = jax.ShapeDtypeStruct((ROWS, width), F32)
    whole = pl.BlockSpec((ROWS, width), lambda k: (0, 0))
    return pl.pallas_call(
        project_kernel,
        grid=(depth // part,),
        in_specs=[
            pl.BlockSpec(memory_space=pltpu.SMEM),
            pl.BlockSpec((2, ROWS), lambda k: (0, 0)),
            pl.BlockSpec((2 * ROWS, part), lambda k: (0, k)),
            pl.BlockSpec((1, part), lambda k: (0, k)),
            pl.BlockSpec((part, QW), lambda k: (k, 0)),
            pl.BlockSpec((part, HD), lambda k: (k, 0)),
            pl.BlockSpec((part, HD), lambda k: (k, 0)),
        ],
        out_specs=[whole, whole],
        out_shape=[out, out],
        scratch_shapes=[pltpu.VMEM((2 * ROWS, HD), F32)],
        compiler_params=params(),
        cost_estimate=pl.CostEstimate(
            flops=2 * 2 * ROWS * depth * width, bytes_accessed=14 * 2**20, transcendentals=0
        ),
    )(span, inverse, hidden, gain, w_query, w_key, w_value)


def spread_kernel(
    home_ref,
    me_ref,
    keep_ref,
    came_ref,
    bias_ref,
    cos_ref,
    sin_ref,
    length_ref,
    ids_ref,
    out0_ref,
    out1_ref,
    out2_ref,
    out3_ref,
    target_ref,
):
    ids = ids_ref[...]
    owner = jnp.zeros_like(ids)
    for prompt in range(HOLDERS):
        owner = jnp.where(ids == prompt, home_ref[prompt], owner)
    owner_column = to_column(owner.astype(F32))
    square = (ROWS, ROWS)
    earlier = lax.broadcasted_iota(jnp.int32, square, 0) < lane_ids(square)
    same = jnp.broadcast_to(owner_column, square) == jnp.broadcast_to(owner.astype(F32), square)
    rank = jnp.sum(jnp.where(earlier & same, 1.0, 0.0), axis=0, keepdims=True).astype(jnp.int32)
    target = (owner ^ me_ref[0]) * CAP + rank
    target_ref[...] = target
    placing = jnp.where(
        lax.broadcasted_iota(jnp.int32, (SLOTS, ROWS), 0) == jnp.broadcast_to(target, (SLOTS, ROWS)),
        1.0,
        0.0,
    ).astype(BF16)
    cosine = cos_ref[...]
    sine = sin_ref[...]
    outs = (out0_ref, out1_ref, out2_ref, out3_ref)
    for head in range(HEADS + 3):
        at = head * HD
        if head == HEADS:
            rows = length_ref[...]
        else:
            source = at if head < HEADS else at - HD
            part = slice(source, source + HD)
            total = keep_ref[:, part] + came_ref[:, part] + bias_ref[:, part]
            if head < HEADS + 2:
                half = HD // 2
                swapped = jnp.concatenate([total[:, half:], total[:, :half]], axis=1)
                total = total * cosine + swapped * sine
            rows = total.astype(BF16)
        placed = jnp.dot(placing, rows, preferred_element_type=F32).astype(BF16)
        placed = placed.astype(F32).reshape(HOLDERS, CAP, HD)
        for index, out_ref in enumerate(outs):
            out_ref[:, :, at : at + HD] = placed[2 * index : 2 * index + 2].astype(BF16)


def spread(home, me, keep, came, bias, cosine, sine, lengths, ids):
    block = jax.ShapeDtypeStruct((2, CAP, ROW_WIDTH), BF16)
    smem = pl.BlockSpec(memory_space=pltpu.SMEM)
    vmem = pl.BlockSpec(memory_space=pltpu.VMEM)
    return pl.pallas_call(
        spread_kernel,
        in_specs=[smem, smem] + [vmem] * 7,
        out_specs=[vmem] * 5,
        out_shape=[block] * 4 + [jax.ShapeDtypeStruct((1, ROWS), jnp.int32)],
        compiler_params=params(),
        cost_estimate=pl.CostEstimate(
            flops=2 * SLOTS * ROWS * ROW_WIDTH, bytes_accessed=2 * 2**20, transcendentals=0
        ),
    )(home, me, keep, came, bias, cosine, sine, lengths, ids)


NT = (((1,), (1,)), ((), ()))


def reply_kernel(where_ref, parity_ref, rows_ref, keys_ref, values_ref, out_ref, log_ref, wide_ref):
    wide_ref[...] = rows_ref[0, :, 0:KEY_AT].astype(F32)
    group = 8
    lanes = lane_ids((group, HD))
    lines = lax.broadcasted_iota(jnp.int32, (group, HD), 0)
    for part in range(CAP // group):
        slots = slice(part * group, (part + 1) * group)
        visible = lanes.astype(F32) < wide_ref[slots, LENGTH_AT : LENGTH_AT + HD]
        stacked = jnp.concatenate(
            [wide_ref[slots, head * HD : (head + 1) * HD] for head in range(HEADS)], axis=0
        ).astype(BF16)
        keys = keys_ref[0, slots].reshape(group * HD, HD)
        values = values_ref[0, slots].reshape(group * HD, HD)
        scores = lax.dot_general(stacked, keys, NT, preferred_element_type=F32)
        weights = []
        sums = []
        logs = jnp.zeros((group, HD), F32)
        for head in range(HEADS):
            mine = slice(head * group, (head + 1) * group)
            own = scores[mine, 0:HD]
            for slot in range(1, group):
                own = jnp.where(lines == slot, scores[mine, slot * HD : (slot + 1) * HD], own)
            own = jnp.where(visible, own, MASKED)
            highest = jnp.max(own, axis=1, keepdims=True)
            weight = jnp.exp2((own - highest) * SCALE)
            total = jnp.sum(weight, axis=1, keepdims=True)
            sums.append(total)
            logs = jnp.where(lanes == head, highest * SCALE + jnp.log2(total), logs)
            weights.append(
                jnp.concatenate(
                    [jnp.where(lines == slot, weight, 0.0) for slot in range(group)], axis=1
                )
            )
        mixed = jnp.dot(
            jnp.concatenate(weights, axis=0).astype(BF16), values, preferred_element_type=F32
        )
        for head in range(HEADS):
            out_ref[0, slots, head * HD : (head + 1) * HD] = (
                mixed[head * group : (head + 1) * group] / sums[head]
            )
        log_ref[0, slots, :] = logs


def reply(where, parity, rows, keys, values):
    quarter = 4
    cached = pl.BlockSpec((1, CAP, HD, HD), lambda b, w, q: (2 * b + q[0], 0, 0, 0))
    return pl.pallas_call(
        reply_kernel,
        grid_spec=pltpu.PrefetchScalarGridSpec(
            num_scalar_prefetch=2,
            grid=(quarter,),
            in_specs=[
                pl.BlockSpec((1, CAP, rows.shape[2]), lambda b, w, q: (w[b], 0, 0)),
                cached,
                cached,
            ],
            out_specs=[
                pl.BlockSpec((1, CAP, QW), lambda b, w, q: (b, 0, 0)),
                pl.BlockSpec((1, CAP, HD), lambda b, w, q: (b, 0, 0)),
            ],
            scratch_shapes=[pltpu.VMEM((CAP, KEY_AT), F32)],
        ),
        out_shape=[
            jax.ShapeDtypeStruct((quarter, CAP, QW), F32),
            jax.ShapeDtypeStruct((quarter, CAP, HD), F32),
        ],
        compiler_params=params(),
        cost_estimate=pl.CostEstimate(
            flops=2 * 10**9, bytes_accessed=8 * 2**20, transcendentals=10**6
        ),
    )(where, parity, rows, keys, values)


def merge_in(out_ref, log_ref, at, other_out, other_log):
    held = log_ref[at]
    highest = jnp.maximum(held, other_log)
    mine = jnp.exp2(held - highest)
    theirs = jnp.exp2(other_log - highest)
    total = mine + theirs
    log_ref[at] = highest + jnp.log2(total)
    mine = mine / total
    theirs = theirs / total
    for head in range(HEADS):
        part = slice(head * HD, (head + 1) * HD)
        out_ref[at, :, part] = (
            out_ref[at, :, part] * mine[:, head : head + 1]
            + other_out(part) * theirs[:, head : head + 1]
        )


def prefix_kernel(
    own,
    where_ref,
    rows_ref,
    keys_ref,
    values_ref,
    reply_ref,
    reply_log_ref,
    *refs,
):
    if own:
        out_ref, log_ref, query_ref, score_ref = refs
    else:
        sent_ref, query_ref, score_ref, out_ref, log_ref = refs
    span = 512
    tokens = keys_ref.shape[0]
    units = 2
    unit_heads = HEADS // units
    unit_rows = unit_heads * SLOTS
    for head in range(HEADS):
        rows = rows_ref[:, :, head * HD : (head + 1) * HD].astype(F32)
        query_ref[head * SLOTS : (head + 1) * SLOTS, :] = rows.reshape(SLOTS, HD).astype(BF16)
    block_lanes = lane_ids((HOLDERS, CAP, HD))
    logs = jnp.zeros((HOLDERS, CAP, HD), F32)
    for unit in range(units):
        queries = query_ref.at[unit * unit_rows : (unit + 1) * unit_rows]

        def score(step, highest):
            start = pl.multiple_of(step * span, span)
            scores = lax.dot_general(
                queries[...], keys_ref[pl.ds(start, span), :], NT, preferred_element_type=F32
            )
            score_ref[step] = scores
            for piece in range(span // HD):
                highest = jnp.maximum(highest, scores[:, piece * HD : (piece + 1) * HD])
            return highest

        highest = lax.fori_loop(
            0, tokens // span, score, jnp.full((unit_rows, HD), MASKED, F32)
        )
        highest = jnp.max(highest, axis=1, keepdims=True)

        def mix(step, carried):
            total, mixed = carried
            start = pl.multiple_of(step * span, span)
            weights = jnp.exp2((score_ref[step] - highest) * SCALE)
            for piece in range(span // HD):
                total = total + weights[:, piece * HD : (piece + 1) * HD]
            mixed = mixed + jnp.dot(
                weights.astype(BF16), values_ref[pl.ds(start, span), :], preferred_element_type=F32
            )
            return total, mixed

        empty = jnp.zeros((unit_rows, HD), F32)
        total, mixed = lax.fori_loop(0, tokens // span, mix, (empty, empty))
        total = jnp.sum(total, axis=1, keepdims=True)
        mixed = mixed / total
        log = jnp.broadcast_to(highest * SCALE + jnp.log2(total), (unit_rows, HD))
        for index in range(unit_heads):
            head = unit * unit_heads + index
            mine = slice(index * SLOTS, (index + 1) * SLOTS)
            out_ref[:, :, head * HD : (head + 1) * HD] = mixed[mine].reshape(HOLDERS, CAP, HD)
            logs = jnp.where(block_lanes == head, log[mine].reshape(HOLDERS, CAP, HD), logs)
    log_ref[...] = logs
    for index in range(reply_ref.shape[0]):
        merge_in(
            out_ref,
            log_ref,
            where_ref[index],
            lambda part: reply_ref[index, :, part],
            reply_log_ref[index],
        )
    if own:
        lanes = lane_ids((CAP, HD))
        for block in range(HOLDERS):
            key = rows_ref[block, :, KEY_AT : KEY_AT + HD].astype(F32)
            value = rows_ref[block, :, VALUE_AT : VALUE_AT + HD].astype(F32)
            logs = jnp.zeros((CAP, HD), F32)
            for head in range(HEADS):
                query = rows_ref[block, :, head * HD : (head + 1) * HD].astype(F32)
                score = jnp.sum(query * key, axis=1, keepdims=True) * SCALE
                logs = jnp.where(lanes == head, score, logs)
            merge_in(out_ref, log_ref, block, lambda part: value, logs)
    else:
        log = log_ref[...]
        high = log.astype(BF16).astype(F32)
        middle = (log - high).astype(BF16).astype(F32)
        low = log - high - middle
        packed = jnp.where(block_lanes < HEADS, high, 0.0)
        for index, piece in ((1, middle), (2, low)):
            moved = jnp.concatenate([piece[:, :, HD - 8 * index :], piece[:, :, : HD - 8 * index]], axis=2)
            here = (block_lanes >= 8 * index) & (block_lanes < 8 * index + 8)
            packed = jnp.where(here, moved, packed)
        sent_ref[:, :, 0:QW] = out_ref[...].astype(BF16)
        sent_ref[:, :, QW:] = packed.astype(BF16)


def prefix(own, where, rows, keys, values, reply_out, reply_log):
    smem = pl.BlockSpec(memory_space=pltpu.SMEM)
    vmem = pl.BlockSpec(memory_space=pltpu.VMEM)
    out = (HOLDERS, CAP, QW)
    log = (HOLDERS, CAP, HD)
    scratch = [
        pltpu.VMEM((HEADS * SLOTS, HD), BF16),
        pltpu.VMEM((keys.shape[0] // 512, HEADS * SLOTS // 2, 512), F32),
    ]
    if own:
        out_shape = [jax.ShapeDtypeStruct(out, F32), jax.ShapeDtypeStruct(log, F32)]
    else:
        out_shape = [jax.ShapeDtypeStruct((HOLDERS, CAP, QW + HD), BF16)]
        scratch += [pltpu.VMEM(out, F32), pltpu.VMEM(log, F32)]
    work = HEADS * SLOTS * keys.shape[0]
    return pl.pallas_call(
        partial(prefix_kernel, own),
        in_specs=[smem] + [vmem] * 5,
        out_specs=[vmem] * len(out_shape),
        out_shape=out_shape,
        scratch_shapes=scratch,
        compiler_params=params(),
        cost_estimate=pl.CostEstimate(
            flops=4 * work * HD, bytes_accessed=4 * 2**20, transcendentals=work
        ),
    )(where, rows, keys, values, reply_out, reply_log)


def combine_kernel(out_ref, log_ref, came_ref, out0_ref, out1_ref, out2_ref, out3_ref):
    for block in range(HOLDERS):
        packed = came_ref[block, :, QW:].astype(F32)
        came_log = packed
        for index in (1, 2):
            came_log = came_log + jnp.concatenate(
                [packed[:, 8 * index :], packed[:, : 8 * index]], axis=1
            )
        held = log_ref[block]
        highest = jnp.maximum(held, came_log)
        mine = jnp.exp2(held - highest)
        theirs = jnp.exp2(came_log - highest)
        total = mine + theirs
        mine = mine / total
        theirs = theirs / total
        target = (out0_ref, out1_ref, out2_ref, out3_ref)[block // 2]
        for head in range(HEADS):
            part = slice(head * HD, (head + 1) * HD)
            target[block % 2, :, part] = (
                out_ref[block, :, part] * mine[:, head : head + 1]
                + came_ref[block, :, part].astype(F32) * theirs[:, head : head + 1]
            ).astype(BF16)


def combine(out, log, came):
    vmem = pl.BlockSpec(memory_space=pltpu.VMEM)
    return pl.pallas_call(
        combine_kernel,
        in_specs=[vmem] * 3,
        out_specs=[vmem] * 4,
        out_shape=[jax.ShapeDtypeStruct((2, CAP, QW), BF16)] * 4,
        compiler_params=params(),
        cost_estimate=pl.CostEstimate(flops=10**6, bytes_accessed=2 * 2**20, transcendentals=10**5),
    )(out, log, came)


def unplace_kernel(target_ref, near0_ref, near1_ref, near2_ref, near3_ref, far_ref, out_ref, rows_ref):
    for index, near in enumerate((near0_ref, near1_ref, near2_ref, near3_ref)):
        rows_ref[2 * index] = near[0].astype(F32)
        rows_ref[2 * index + 1] = far_ref[index].astype(F32)
    rows = rows_ref[...].reshape(SLOTS, QW).astype(BF16)
    target = target_ref[...]
    placing = jnp.where(
        lax.broadcasted_iota(jnp.int32, (SLOTS, ROWS), 0) == jnp.broadcast_to(target, (SLOTS, ROWS)),
        1.0,
        0.0,
    ).astype(BF16)
    out_ref[...] = lax.dot_general(
        placing, rows, (((0,), (0,)), ((), ())), preferred_element_type=F32
    ).astype(BF16)


def unplace(target, nears, far):
    vmem = pl.BlockSpec(memory_space=pltpu.VMEM)
    return pl.pallas_call(
        unplace_kernel,
        in_specs=[vmem] * 6,
        out_specs=vmem,
        out_shape=jax.ShapeDtypeStruct((ROWS, QW), BF16),
        scratch_shapes=[pltpu.VMEM((HOLDERS, CAP, QW), F32)],
        compiler_params=params(),
        cost_estimate=pl.CostEstimate(
            flops=2 * SLOTS * ROWS * QW, bytes_accessed=2**20, transcendentals=0
        ),
    )(target, *nears, far)


def store_kernel(me_ref, span_ref, own_ref, other_ref, out_ref):
    for block in range(HOLDERS):
        origin = me_ref[0] ^ block
        for rows_ref, parity in ((own_ref, span_ref[0]), (other_ref, 1 - span_ref[0])):
            for kind in range(2):
                out_ref[kind, 2 * origin + parity] = rows_ref[block, :, kind * HD : (kind + 1) * HD]


def store(me, span, own, other):
    smem = pl.BlockSpec(memory_space=pltpu.SMEM)
    vmem = pl.BlockSpec(memory_space=pltpu.VMEM)
    return pl.pallas_call(
        store_kernel,
        in_specs=[smem, smem, vmem, vmem],
        out_specs=vmem,
        out_shape=jax.ShapeDtypeStruct((2, 2 * HOLDERS, CAP, HD), BF16),
        compiler_params=params(),
        cost_estimate=pl.CostEstimate(flops=0, bytes_accessed=2**19, transcendentals=0),
    )(me, span, own, other)


def other_pair(values):
    return lax.ppermute(values, "pair", [(0, 1), (1, 0)])


def flip(values, bits):
    return lax.ppermute(values, "memory", [(m, m ^ bits) for m in range(HOLDERS)])


def body(
    hidden,
    norm_gain,
    w_query,
    w_key,
    w_value,
    query_bias,
    key_bias,
    value_bias,
    prefix_keys,
    prefix_values,
    reply_keys,
    reply_values,
    reply_length,
    prefix_ids,
    prompt_home,
):
    me = lax.axis_index("memory").astype(jnp.int32).reshape(1)
    span = lax.axis_index("pair").astype(jnp.int32).reshape(1)

    widened = hidden.astype(F32)
    squares = jnp.sum(widened * widened, axis=1)
    squares = squares + other_pair(squares)
    inverse = lax.rsqrt(squares / D + EPSILON).reshape(2, ROWS)
    keep, send = project(
        span, inverse, hidden, norm_gain.reshape(1, -1), w_query, w_key, w_value
    )
    came = other_pair(send)

    half = HD // 2
    ladder = jnp.arange(half, dtype=F32) * (2.0 / HD)
    frequency = jnp.power(ROPE_BASE, -ladder)
    angles = (PREFIX + reply_length).astype(F32)[:, None] * frequency
    cosine = jnp.cos(angles)
    sine = jnp.sin(angles)
    cosine = jnp.concatenate([cosine, cosine], axis=1)
    sine = jnp.concatenate([-sine, sine], axis=1)
    lengths = jnp.broadcast_to(reply_length.astype(BF16)[:, None], (ROWS, HD))
    bias = jnp.concatenate([query_bias, key_bias, value_bias]).astype(F32).reshape(1, -1)
    *blocks, target = spread(
        prompt_home, me, keep, came, bias, cosine, sine, lengths, prefix_ids.reshape(1, ROWS)
    )

    near = [blocks[0]] + [flip(blocks[step], 2 * step) for step in range(1, 4)]
    far = flip(jnp.stack([block[1] for block in near]), 1)
    rows = jnp.stack([piece for step in range(4) for piece in (near[step][0], far[step])])
    partner_rows = other_pair(rows[:, :, :KEY_AT])
    fresh = rows[:, :, KEY_AT:]
    partner_fresh = other_pair(fresh)

    origin = 4 * span[0] + jnp.arange(4, dtype=jnp.int32)
    where = me[0] ^ origin
    caches = (8, CAP, HD, HD)
    keys = reply_keys.reshape(caches)
    values = reply_values.reshape(caches)
    prompt_keys = prefix_keys[0]
    prompt_values = prefix_values[0]
    own_reply = reply(where, span, rows, keys, values)
    out, log = prefix(True, where, rows, prompt_keys, prompt_values, *own_reply)
    partner_reply = reply(where, 1 - span, partner_rows, keys, values)
    (sent,) = prefix(False, where, partner_rows, prompt_keys, prompt_values, *partner_reply)
    came = other_pair(sent)
    merged = combine(out, log, came)

    nears = [merged[0]] + [flip(merged[step], 2 * step) for step in range(1, 4)]
    fars = flip(jnp.stack([block[1] for block in nears]), 1)
    attention = unplace(target, nears, fars)
    stored = store(me, span, fresh, partner_fresh).reshape(2, 1, 2 * SLOTS, HD)
    return attention, stored


def solution(mesh):
    in_specs = (
        P("memory", "pair"),
        P("pair"),
        P("pair", "compute"),
        P("pair", "compute"),
        P("pair", "compute"),
        P("compute"),
        P("compute"),
        P("compute"),
        P("memory", "pair", "compute"),
        P("memory", "pair", "compute"),
        P("memory", "pair", None, "compute"),
        P("memory", "pair", None, "compute"),
        P(("memory", "pair")),
        P(("memory", "pair")),
        P(),
    )
    out_specs = (P(("memory", "pair"), "compute"), P(None, "memory", None, "compute"))
    return jax.shard_map(body, mesh=mesh, in_specs=in_specs, out_specs=out_specs, check_vma=False)
```

```python
from functools import partial

import jax
import jax.numpy as jnp
from jax import lax
from jax.experimental import pallas as pl
from jax.experimental.pallas import tpu as pltpu
from jax.sharding import PartitionSpec as P

D = 8192
HD = 128
PREFIX = 8192
EPSILON = 1e-06
ROPE_BASE = 1000000.0
MASKED = -1e30
ROWS = 128
HOLDERS = 8
CAP = 24
HEADS = 8
QW = HEADS * HD
SLOTS = HOLDERS * CAP
BLOCK = 256
LENGTH_AT = QW
KEY_AT = QW + HD
VALUE_AT = QW + 2 * HD
ROW_WIDTH = QW + 3 * HD
SCALE = 1.4426950408889634 / HD**0.5
F32 = jnp.float32
BF16 = jnp.bfloat16


def params(mebibytes):
    return pltpu.CompilerParams(vmem_limit_bytes=mebibytes * 2**20)


def lane_ids(shape):
    return lax.broadcasted_iota(jnp.int32, shape, len(shape) - 1)


def to_column(row):
    size = row.shape[1]
    spread = jnp.broadcast_to(row, (size, size))
    diagonal = lax.broadcasted_iota(jnp.int32, (size, size), 0) == lane_ids((size, size))
    return jnp.sum(jnp.where(diagonal, spread, jnp.zeros_like(spread)), axis=1, keepdims=True)


def project_kernel(
    span_ref,
    mine_ref,
    theirs_ref,
    hidden_ref,
    gain_ref,
    wq_ref,
    wk_ref,
    wv_ref,
    keep_ref,
    send_ref,
    normed_ref,
):
    span = span_ref[0]
    inverse = lax.rsqrt((mine_ref[...] + theirs_ref[...]) / D + EPSILON)
    first = to_column(inverse[0:1, :])
    second = to_column(inverse[1:2, :])
    scales = (jnp.where(span == 0, first, second), jnp.where(span == 0, second, first))
    gain = gain_ref[...].astype(F32).reshape(1, -1)
    for where, start in enumerate((span * ROWS, (1 - span) * ROWS)):
        rows = hidden_ref[pl.ds(pl.multiple_of(start, ROWS), ROWS), :].astype(F32)
        normed = rows * scales[where] * gain
        normed_ref[where * ROWS : (where + 1) * ROWS, :] = normed.astype(BF16)
    pieces = [(at, wq_ref.at[:, at : at + 256]) for at in range(0, QW, 256)]
    pieces += [(QW, wk_ref), (QW + HD, wv_ref)]
    for at, w_ref in pieces:
        part = slice(at, at + w_ref.shape[1])
        total = jnp.dot(normed_ref[...], w_ref[...], preferred_element_type=F32)
        keep_ref[:, part] = total[:ROWS]
        send_ref[:, part] = total[ROWS:]


def project(span, mine, theirs, hidden, gain, w_query, w_key, w_value):
    depth = hidden.shape[1]
    width = QW + 2 * HD
    out = jax.ShapeDtypeStruct((ROWS, width), F32)
    vmem = pl.BlockSpec(memory_space=pltpu.VMEM)
    return pl.pallas_call(
        project_kernel,
        in_specs=[pl.BlockSpec(memory_space=pltpu.SMEM)] + [vmem] * 7,
        out_specs=[vmem] * 2,
        out_shape=[out, out],
        scratch_shapes=[pltpu.VMEM((2 * ROWS, depth), BF16)],
        compiler_params=params(20),
        cost_estimate=pl.CostEstimate(
            flops=2 * 2 * ROWS * depth * width, bytes_accessed=14 * 2**20, transcendentals=0
        ),
    )(span, mine, theirs, hidden, gain, w_query, w_key, w_value)


def spread_kernel(
    home_ref,
    me_ref,
    keep_ref,
    came_ref,
    bias_ref,
    cos_ref,
    sin_ref,
    length_ref,
    ids_ref,
    out0_ref,
    out1_ref,
    out2_ref,
    out3_ref,
    target_ref,
):
    ids = ids_ref[...]
    owner = jnp.zeros_like(ids)
    for prompt in range(HOLDERS):
        owner = jnp.where(ids == prompt, home_ref[prompt], owner)
    owner_column = to_column(owner.astype(F32))
    square = (ROWS, ROWS)
    earlier = lax.broadcasted_iota(jnp.int32, square, 0) < lane_ids(square)
    same = jnp.broadcast_to(owner_column, square) == jnp.broadcast_to(owner.astype(F32), square)
    rank = jnp.sum(jnp.where(earlier & same, 1.0, 0.0), axis=0, keepdims=True).astype(jnp.int32)
    target = (owner ^ me_ref[0]) * CAP + rank
    target_ref[...] = target
    placing = jnp.where(
        lax.broadcasted_iota(jnp.int32, (SLOTS, ROWS), 0) == jnp.broadcast_to(target, (SLOTS, ROWS)),
        1.0,
        0.0,
    ).astype(BF16)
    cosine = cos_ref[...]
    sine = sin_ref[...]
    outs = (out0_ref, out1_ref, out2_ref, out3_ref)
    for head in range(HEADS + 3):
        at = head * HD
        if head == HEADS:
            rows = jnp.broadcast_to(to_column(length_ref[...].astype(F32)), square).astype(BF16)
        else:
            source = at if head < HEADS else at - HD
            part = slice(source, source + HD)
            total = keep_ref[:, part] + came_ref[:, part] + bias_ref[:, part]
            if head < HEADS + 2:
                half = HD // 2
                swapped = jnp.concatenate([total[:, half:], total[:, :half]], axis=1)
                total = total * cosine + swapped * sine
            rows = total.astype(BF16)
        placed = jnp.dot(placing, rows, preferred_element_type=F32).astype(BF16)
        placed = placed.astype(F32).reshape(HOLDERS, CAP, HD)
        for index, out_ref in enumerate(outs):
            out_ref[:, :, at : at + HD] = placed[2 * index : 2 * index + 2].astype(BF16)


def spread(home, me, keep, came, bias, cosine, sine, lengths, ids):
    block = jax.ShapeDtypeStruct((2, CAP, ROW_WIDTH), BF16)
    smem = pl.BlockSpec(memory_space=pltpu.SMEM)
    vmem = pl.BlockSpec(memory_space=pltpu.VMEM)
    return pl.pallas_call(
        spread_kernel,
        in_specs=[smem, smem] + [vmem] * 7,
        out_specs=[vmem] * 5,
        out_shape=[block] * 4 + [jax.ShapeDtypeStruct((1, ROWS), jnp.int32)],
        compiler_params=params(8),
        cost_estimate=pl.CostEstimate(
            flops=2 * SLOTS * ROWS * ROW_WIDTH, bytes_accessed=2 * 2**20, transcendentals=0
        ),
    )(home, me, keep, came, bias, cosine, sine, lengths, ids)


NT = (((1,), (1,)), ((), ()))


def reply_kernel(where_ref, parity_ref, rows_ref, keys_ref, values_ref, out_ref, log_ref, wide_ref):
    wide_ref[...] = rows_ref[0, :, 0:KEY_AT].astype(F32)
    group = 8
    parts = CAP // group
    lanes = lane_ids((group, HD))
    lines = lax.broadcasted_iota(jnp.int32, (group, HD), 0)
    scores = []
    for part in range(parts):
        slots = slice(part * group, (part + 1) * group)
        stacked = jnp.concatenate(
            [wide_ref[slots, head * HD : (head + 1) * HD] for head in range(HEADS)], axis=0
        ).astype(BF16)
        keys = keys_ref[0, slots].reshape(group * HD, HD)
        scores.append(lax.dot_general(stacked, keys, NT, preferred_element_type=F32))
    weights = []
    totals = []
    for part in range(parts):
        slots = slice(part * group, (part + 1) * group)
        visible = lanes.astype(F32) < wide_ref[slots, LENGTH_AT : LENGTH_AT + HD]
        visible = jnp.concatenate([visible] * HEADS, axis=0)
        own = jnp.zeros((HEADS * group, HD), F32)
        line = lax.broadcasted_iota(jnp.int32, own.shape, 0) % group
        for slot in range(group):
            own = jnp.where(line == slot, scores[part][:, slot * HD : (slot + 1) * HD], own)
        own = jnp.where(visible, own, MASKED)
        highest = jnp.max(own, axis=1, keepdims=True)
        weight = jnp.exp2((own - highest) * SCALE)
        total = jnp.sum(weight, axis=1, keepdims=True)
        totals.append(total)
        log = jnp.broadcast_to(highest * SCALE + jnp.log2(total), own.shape)
        logs = jnp.zeros((group, HD), F32)
        for head in range(HEADS):
            logs = jnp.where(lanes == head, log[head * group : (head + 1) * group], logs)
        log_ref[0, slots, :] = logs
        weights.append(
            jnp.concatenate(
                [jnp.where(line == slot, weight, 0.0).astype(BF16) for slot in range(group)], axis=1
            )
        )
    for part in range(parts):
        slots = slice(part * group, (part + 1) * group)
        values = values_ref[0, slots].reshape(group * HD, HD)
        mixed = jnp.dot(weights[part], values, preferred_element_type=F32) / totals[part]
        for head in range(HEADS):
            out_ref[0, slots, head * HD : (head + 1) * HD] = mixed[head * group : (head + 1) * group]


def reply(where, parity, rows, keys, values):
    quarter = 4
    cached = pl.BlockSpec((1, CAP, HD, HD), lambda b, w, q: (2 * b + q[0], 0, 0, 0))
    return pl.pallas_call(
        reply_kernel,
        grid_spec=pltpu.PrefetchScalarGridSpec(
            num_scalar_prefetch=2,
            grid=(quarter,),
            in_specs=[
                pl.BlockSpec((1, CAP, rows.shape[2]), lambda b, w, q: (w[b], 0, 0)),
                cached,
                cached,
            ],
            out_specs=[
                pl.BlockSpec((1, CAP, QW), lambda b, w, q: (b, 0, 0)),
                pl.BlockSpec((1, CAP, HD), lambda b, w, q: (b, 0, 0)),
            ],
            scratch_shapes=[pltpu.VMEM((CAP, KEY_AT), F32)],
        ),
        out_shape=[
            jax.ShapeDtypeStruct((quarter, CAP, QW), F32),
            jax.ShapeDtypeStruct((quarter, CAP, HD), F32),
        ],
        compiler_params=params(12),
        cost_estimate=pl.CostEstimate(
            flops=2 * 10**9, bytes_accessed=8 * 2**20, transcendentals=10**6
        ),
    )(where, parity, rows, keys, values)


def merge_in(out_ref, log_ref, at, other_out, other_log):
    held = log_ref[at]
    highest = jnp.maximum(held, other_log)
    mine = jnp.exp2(held - highest)
    theirs = jnp.exp2(other_log - highest)
    total = mine + theirs
    log_ref[at] = highest + jnp.log2(total)
    mine = mine / total
    theirs = theirs / total
    for head in range(HEADS):
        part = slice(head * HD, (head + 1) * HD)
        out_ref[at, :, part] = (
            out_ref[at, :, part] * mine[:, head : head + 1]
            + other_out(part) * theirs[:, head : head + 1]
        )


def prefix_kernel(
    own,
    where_ref,
    rows_ref,
    keys_ref,
    values_ref,
    reply_ref,
    reply_log_ref,
    *refs,
):
    if own:
        out_ref, log_ref, *scratch = refs
    else:
        sent_ref, *scratch, out_ref, log_ref = refs
    query_ref, score0_ref, score1_ref, mixed_ref, logs_ref = scratch
    for head in range(HEADS):
        rows = rows_ref[:, :, head * HD : (head + 1) * HD].astype(F32)
        query_ref[head * SLOTS : (head + 1) * SLOTS, :] = rows.reshape(SLOTS, HD).astype(BF16)
    held = (score0_ref, score1_ref)
    total_rows = HEADS * SLOTS

    def score(block):
        queries = query_ref[block * BLOCK : (block + 1) * BLOCK]
        held[block % 2][...] = lax.dot_general(
            queries, keys_ref[...], NT, preferred_element_type=F32
        )

    score(0)
    for block in range(total_rows // BLOCK):
        here = slice(block * BLOCK, (block + 1) * BLOCK)
        scores = held[block % 2][...]
        highest = jnp.max(scores, axis=1, keepdims=True)
        if block + 1 < total_rows // BLOCK:
            score(block + 1)
        weights = jnp.exp2((scores - highest) * SCALE)
        total = jnp.sum(weights, axis=1, keepdims=True)
        mixed = jnp.dot(weights.astype(BF16), values_ref[...], preferred_element_type=F32)
        mixed_ref[here] = mixed / total
        logs_ref[here] = jnp.broadcast_to(highest * SCALE + jnp.log2(total), (BLOCK, HD))
    block_lanes = lane_ids((HOLDERS, CAP, HD))
    logs = jnp.zeros((HOLDERS, CAP, HD), F32)
    for head in range(HEADS):
        mine = slice(head * SLOTS, (head + 1) * SLOTS)
        out_ref[:, :, head * HD : (head + 1) * HD] = mixed_ref[mine].reshape(HOLDERS, CAP, HD)
        logs = jnp.where(block_lanes == head, logs_ref[mine].reshape(HOLDERS, CAP, HD), logs)
    log_ref[...] = logs
    for index in range(reply_ref.shape[0]):
        merge_in(
            out_ref,
            log_ref,
            where_ref[index],
            lambda part: reply_ref[index, :, part],
            reply_log_ref[index],
        )
    if own:
        lanes = lane_ids((CAP, HD))
        for block in range(HOLDERS):
            key = rows_ref[block, :, KEY_AT : KEY_AT + HD].astype(F32)
            value = rows_ref[block, :, VALUE_AT : VALUE_AT + HD].astype(F32)
            logs = jnp.zeros((CAP, HD), F32)
            for head in range(HEADS):
                query = rows_ref[block, :, head * HD : (head + 1) * HD].astype(F32)
                score = jnp.sum(query * key, axis=1, keepdims=True) * SCALE
                logs = jnp.where(lanes == head, score, logs)
            merge_in(out_ref, log_ref, block, lambda part: value, logs)
    else:
        log = log_ref[...]
        high = log.astype(BF16).astype(F32)
        middle = (log - high).astype(BF16).astype(F32)
        low = log - high - middle
        packed = jnp.where(block_lanes < HEADS, high, 0.0)
        for index, piece in ((1, middle), (2, low)):
            moved = jnp.concatenate([piece[:, :, HD - 8 * index :], piece[:, :, : HD - 8 * index]], axis=2)
            here = (block_lanes >= 8 * index) & (block_lanes < 8 * index + 8)
            packed = jnp.where(here, moved, packed)
        sent_ref[:, :, 0:QW] = out_ref[...].astype(BF16)
        sent_ref[:, :, QW:] = packed.astype(BF16)


def prefix(own, where, rows, keys, values, reply_out, reply_log):
    smem = pl.BlockSpec(memory_space=pltpu.SMEM)
    vmem = pl.BlockSpec(memory_space=pltpu.VMEM)
    out = (HOLDERS, CAP, QW)
    log = (HOLDERS, CAP, HD)
    scratch = [
        pltpu.VMEM((HEADS * SLOTS, HD), BF16),
        pltpu.VMEM((BLOCK, keys.shape[0]), F32),
        pltpu.VMEM((BLOCK, keys.shape[0]), F32),
        pltpu.VMEM((HEADS * SLOTS, HD), F32),
        pltpu.VMEM((HEADS * SLOTS, HD), F32),
    ]
    if own:
        out_shape = [jax.ShapeDtypeStruct(out, F32), jax.ShapeDtypeStruct(log, F32)]
    else:
        out_shape = [jax.ShapeDtypeStruct((HOLDERS, CAP, QW + HD), BF16)]
        scratch += [pltpu.VMEM(out, F32), pltpu.VMEM(log, F32)]
    work = HEADS * SLOTS * keys.shape[0]
    return pl.pallas_call(
        partial(prefix_kernel, own),
        in_specs=[smem] + [vmem] * 5,
        out_specs=[vmem] * len(out_shape),
        out_shape=out_shape,
        scratch_shapes=scratch,
        compiler_params=params(24),
        cost_estimate=pl.CostEstimate(
            flops=4 * work * HD, bytes_accessed=4 * 2**20, transcendentals=work
        ),
    )(where, rows, keys, values, reply_out, reply_log)


def combine_kernel(out_ref, log_ref, came_ref, out0_ref, out1_ref, out2_ref, out3_ref):
    for block in range(HOLDERS):
        packed = came_ref[block, :, QW:].astype(F32)
        came_log = packed
        for index in (1, 2):
            came_log = came_log + jnp.concatenate(
                [packed[:, 8 * index :], packed[:, : 8 * index]], axis=1
            )
        held = log_ref[block]
        highest = jnp.maximum(held, came_log)
        mine = jnp.exp2(held - highest)
        theirs = jnp.exp2(came_log - highest)
        total = mine + theirs
        mine = mine / total
        theirs = theirs / total
        target = (out0_ref, out1_ref, out2_ref, out3_ref)[block // 2]
        for head in range(HEADS):
            part = slice(head * HD, (head + 1) * HD)
            target[block % 2, :, part] = (
                out_ref[block, :, part] * mine[:, head : head + 1]
                + came_ref[block, :, part].astype(F32) * theirs[:, head : head + 1]
            ).astype(BF16)


def combine(out, log, came):
    vmem = pl.BlockSpec(memory_space=pltpu.VMEM)
    return pl.pallas_call(
        combine_kernel,
        in_specs=[vmem] * 3,
        out_specs=[vmem] * 4,
        out_shape=[jax.ShapeDtypeStruct((2, CAP, QW), BF16)] * 4,
        compiler_params=params(6),
        cost_estimate=pl.CostEstimate(flops=10**6, bytes_accessed=2 * 2**20, transcendentals=10**5),
    )(out, log, came)


def unplace_kernel(target_ref, near0_ref, near1_ref, near2_ref, near3_ref, far_ref, out_ref, rows_ref):
    for index, near in enumerate((near0_ref, near1_ref, near2_ref, near3_ref)):
        rows_ref[2 * index] = near[0].astype(F32)
        rows_ref[2 * index + 1] = far_ref[index].astype(F32)
    rows = rows_ref[...].reshape(SLOTS, QW).astype(BF16)
    target = target_ref[...]
    placing = jnp.where(
        lax.broadcasted_iota(jnp.int32, (SLOTS, ROWS), 0) == jnp.broadcast_to(target, (SLOTS, ROWS)),
        1.0,
        0.0,
    ).astype(BF16)
    out_ref[...] = lax.dot_general(
        placing, rows, (((0,), (0,)), ((), ())), preferred_element_type=F32
    ).astype(BF16)


def unplace(target, nears, far):
    vmem = pl.BlockSpec(memory_space=pltpu.VMEM)
    return pl.pallas_call(
        unplace_kernel,
        in_specs=[vmem] * 6,
        out_specs=vmem,
        out_shape=jax.ShapeDtypeStruct((ROWS, QW), BF16),
        scratch_shapes=[pltpu.VMEM((HOLDERS, CAP, QW), F32)],
        compiler_params=params(6),
        cost_estimate=pl.CostEstimate(
            flops=2 * SLOTS * ROWS * QW, bytes_accessed=2**20, transcendentals=0
        ),
    )(target, *nears, far)


def store_kernel(me_ref, span_ref, own_ref, other_ref, out_ref):
    for block in range(HOLDERS):
        origin = me_ref[0] ^ block
        for rows_ref, parity in ((own_ref, span_ref[0]), (other_ref, 1 - span_ref[0])):
            for kind in range(2):
                out_ref[kind, 2 * origin + parity] = rows_ref[block, :, kind * HD : (kind + 1) * HD]


def store(me, span, own, other):
    smem = pl.BlockSpec(memory_space=pltpu.SMEM)
    vmem = pl.BlockSpec(memory_space=pltpu.VMEM)
    return pl.pallas_call(
        store_kernel,
        in_specs=[smem, smem, vmem, vmem],
        out_specs=vmem,
        out_shape=jax.ShapeDtypeStruct((2, 2 * HOLDERS, CAP, HD), BF16),
        compiler_params=params(4),
        cost_estimate=pl.CostEstimate(flops=0, bytes_accessed=2**19, transcendentals=0),
    )(me, span, own, other)


def other_pair(values):
    return lax.ppermute(values, "pair", [(0, 1), (1, 0)])


def flip(values, bits):
    return lax.ppermute(values, "memory", [(m, m ^ bits) for m in range(HOLDERS)])


def body(
    hidden,
    norm_gain,
    w_query,
    w_key,
    w_value,
    query_bias,
    key_bias,
    value_bias,
    prefix_keys,
    prefix_values,
    reply_keys,
    reply_values,
    reply_length,
    prefix_ids,
    prompt_home,
):
    me = lax.axis_index("memory").astype(jnp.int32).reshape(1)
    span = lax.axis_index("pair").astype(jnp.int32).reshape(1)

    widened = hidden.astype(F32)
    squares = jnp.sum(widened * widened, axis=1)
    theirs = other_pair(squares)
    keep, send = project(
        span,
        squares.reshape(2, ROWS),
        theirs.reshape(2, ROWS),
        hidden,
        norm_gain,
        w_query,
        w_key,
        w_value,
    )
    came = other_pair(send)

    half = HD // 2
    ladder = jnp.arange(half, dtype=F32) * (2.0 / HD)
    frequency = jnp.power(ROPE_BASE, -ladder)
    angles = (PREFIX + reply_length).astype(F32)[:, None] * frequency
    cosine = jnp.cos(angles)
    sine = jnp.sin(angles)
    cosine = jnp.concatenate([cosine, cosine], axis=1)
    sine = jnp.concatenate([-sine, sine], axis=1)
    bias = jnp.concatenate([query_bias, key_bias, value_bias]).astype(F32).reshape(1, -1)
    *blocks, target = spread(
        prompt_home, me, keep, came, bias, cosine, sine, reply_length.reshape(1, ROWS), prefix_ids.reshape(1, ROWS)
    )

    near = [blocks[0]] + [flip(blocks[step], 2 * step) for step in range(1, 4)]
    far = flip(jnp.stack([block[1] for block in near]), 1)
    rows = jnp.stack([piece for step in range(4) for piece in (near[step][0], far[step])])
    partner_rows = other_pair(rows[:, :, :KEY_AT])
    fresh = rows[:, :, KEY_AT:]
    partner_fresh = other_pair(fresh)

    origin = 4 * span[0] + jnp.arange(4, dtype=jnp.int32)
    where = me[0] ^ origin
    caches = (8, CAP, HD, HD)
    keys = reply_keys.reshape(caches)
    values = reply_values.reshape(caches)
    prompt_keys = prefix_keys[0]
    prompt_values = prefix_values[0]
    own_reply = reply(where, span, rows, keys, values)
    own_reply, partner_rows, partner_fresh = lax.optimization_barrier(
        (own_reply, partner_rows, partner_fresh)
    )
    stored = store(me, span, fresh, partner_fresh).reshape(2, 1, 2 * SLOTS, HD)
    partner_reply = reply(where, 1 - span, partner_rows, keys, values)
    (sent,) = prefix(False, where, partner_rows, prompt_keys, prompt_values, *partner_reply)
    came = other_pair(sent)
    rows, sent, stored = lax.optimization_barrier((rows, sent, stored))
    out, log = prefix(True, where, rows, prompt_keys, prompt_values, *own_reply)
    merged = combine(out, log, came)

    nears = [merged[0]] + [flip(merged[step], 2 * step) for step in range(1, 4)]
    fars = flip(jnp.stack([block[1] for block in nears]), 1)
    attention = unplace(target, nears, fars)
    return attention, stored


def solution(mesh):
    in_specs = (
        P("memory", "pair"),
        P("pair"),
        P("pair", "compute"),
        P("pair", "compute"),
        P("pair", "compute"),
        P("compute"),
        P("compute"),
        P("compute"),
        P("memory", "pair", "compute"),
        P("memory", "pair", "compute"),
        P("memory", "pair", None, "compute"),
        P("memory", "pair", None, "compute"),
        P(("memory", "pair")),
        P(("memory", "pair")),
        P(),
    )
    out_specs = (P(("memory", "pair"), "compute"), P(None, "memory", None, "compute"))
    return jax.shard_map(body, mesh=mesh, in_specs=in_specs, out_specs=out_specs, check_vma=False)
```

```python
from functools import partial

import jax
import jax.numpy as jnp
from jax import lax
from jax.experimental import pallas as pl
from jax.experimental.pallas import tpu as pltpu
from jax.sharding import PartitionSpec as P

D = 8192
HD = 128
PREFIX = 8192
EPSILON = 1e-06
ROPE_BASE = 1000000.0
MASKED = -1e30
ROWS = 128
HOLDERS = 8
CAP = 24
HEADS = 8
QW = HEADS * HD
SLOTS = HOLDERS * CAP
BLOCK = 256
PIECES = 8
CUT = 768
LENGTH_AT = QW
KEY_AT = QW + HD
VALUE_AT = QW + 2 * HD
ROW_WIDTH = QW + 3 * HD
SCALE = 1.4426950408889634 / HD**0.5
F32 = jnp.float32
BF16 = jnp.bfloat16


def params(mebibytes):
    return pltpu.CompilerParams(vmem_limit_bytes=mebibytes * 2**20)


def lane_ids(shape):
    return lax.broadcasted_iota(jnp.int32, shape, len(shape) - 1)


def to_column(row):
    size = row.shape[1]
    spread = jnp.broadcast_to(row, (size, size))
    diagonal = lax.broadcasted_iota(jnp.int32, (size, size), 0) == lane_ids((size, size))
    return jnp.sum(jnp.where(diagonal, spread, jnp.zeros_like(spread)), axis=1, keepdims=True)


def project_kernel(
    span_ref,
    mine_ref,
    theirs_ref,
    hidden_ref,
    gain_ref,
    wq_ref,
    wk_ref,
    wv_ref,
    keep_ref,
    send0_ref,
    send1_ref,
    rows_ref,
    query_ref,
    key_ref,
    value_ref,
    normed_ref,
    sems,
):
    depth = rows_ref.shape[1]
    step = depth // PIECES
    copies = [pltpu.make_async_copy(hidden_ref, rows_ref, sems.at[0])]
    for piece in range(PIECES):
        part = pl.ds(piece * step, step)
        copies.append(
            pltpu.make_async_copy(wq_ref.at[part], query_ref.at[part], sems.at[1 + piece])
        )
    copies.append(pltpu.make_async_copy(wk_ref, key_ref, sems.at[1 + PIECES]))
    copies.append(pltpu.make_async_copy(wv_ref, value_ref, sems.at[2 + PIECES]))
    for copy in copies:
        copy.start()
    span = span_ref[0]
    inverse = lax.rsqrt((mine_ref[...] + theirs_ref[...]) / D + EPSILON)
    first = to_column(inverse[0:1, :])
    second = to_column(inverse[1:2, :])
    scales = (jnp.where(span == 0, first, second), jnp.where(span == 0, second, first))
    gain = gain_ref[...].astype(F32).reshape(1, -1)
    copies[0].wait()
    for where, start in enumerate((span * ROWS, (1 - span) * ROWS)):
        rows = rows_ref[pl.ds(pl.multiple_of(start, ROWS), ROWS), :].astype(F32)
        normed = rows * scales[where] * gain
        normed_ref[where * ROWS : (where + 1) * ROWS, :] = normed.astype(BF16)

    def add(at, total, fresh):
        width = total.shape[1]
        send_ref, here = (send0_ref, at) if at < CUT else (send1_ref, at - CUT)
        for out_ref, rows, column in ((keep_ref, total[:ROWS], at), (send_ref, total[ROWS:], here)):
            part = slice(column, column + width)
            out_ref[:, part] = rows if fresh else out_ref[:, part] + rows

    for piece in range(PIECES):
        copies[1 + piece].wait()
        part = slice(piece * step, (piece + 1) * step)
        for at in range(0, QW, 256):
            weights = query_ref[part, at : at + 256]
            add(at, jnp.dot(normed_ref[:, part], weights, preferred_element_type=F32), piece == 0)
    for index, w_ref in enumerate((key_ref, value_ref)):
        copies[1 + PIECES + index].wait()
        total = jnp.dot(normed_ref[...], w_ref[...], preferred_element_type=F32)
        add(QW + index * HD, total, True)


def project(span, mine, theirs, hidden, gain, w_query, w_key, w_value):
    depth = hidden.shape[1]
    width = QW + 2 * HD
    vmem = pl.BlockSpec(memory_space=pltpu.VMEM)
    hbm = pl.BlockSpec(memory_space=pltpu.HBM)
    return pl.pallas_call(
        project_kernel,
        in_specs=[pl.BlockSpec(memory_space=pltpu.SMEM), vmem, vmem, hbm, vmem, hbm, hbm, hbm],
        out_specs=[vmem] * 3,
        out_shape=[
            jax.ShapeDtypeStruct((ROWS, width), F32),
            jax.ShapeDtypeStruct((ROWS, CUT), F32),
            jax.ShapeDtypeStruct((ROWS, width - CUT), F32),
        ],
        scratch_shapes=[
            pltpu.VMEM((2 * ROWS, depth), BF16),
            pltpu.VMEM((depth, QW), BF16),
            pltpu.VMEM((depth, HD), BF16),
            pltpu.VMEM((depth, HD), BF16),
            pltpu.VMEM((2 * ROWS, depth), BF16),
            pltpu.SemaphoreType.DMA((3 + PIECES,)),
        ],
        compiler_params=params(56),
        cost_estimate=pl.CostEstimate(
            flops=2 * 2 * ROWS * depth * width, bytes_accessed=14 * 2**20, transcendentals=0
        ),
    )(span, mine, theirs, hidden, gain, w_query, w_key, w_value)


def spread_kernel(
    home_ref,
    me_ref,
    keep_ref,
    came0_ref,
    came1_ref,
    bias_ref,
    cos_ref,
    sin_ref,
    length_ref,
    ids_ref,
    out0_ref,
    out1_ref,
    out2_ref,
    out3_ref,
    target_ref,
):
    ids = ids_ref[...]
    owner = jnp.zeros_like(ids)
    for prompt in range(HOLDERS):
        owner = jnp.where(ids == prompt, home_ref[prompt], owner)
    owner_column = to_column(owner.astype(F32))
    square = (ROWS, ROWS)
    earlier = lax.broadcasted_iota(jnp.int32, square, 0) < lane_ids(square)
    same = jnp.broadcast_to(owner_column, square) == jnp.broadcast_to(owner.astype(F32), square)
    rank = jnp.sum(jnp.where(earlier & same, 1.0, 0.0), axis=0, keepdims=True).astype(jnp.int32)
    target = (owner ^ me_ref[0]) * CAP + rank
    target_ref[...] = target
    placing = jnp.where(
        lax.broadcasted_iota(jnp.int32, (SLOTS, ROWS), 0) == jnp.broadcast_to(target, (SLOTS, ROWS)),
        1.0,
        0.0,
    ).astype(BF16)
    cosine = cos_ref[...]
    sine = sin_ref[...]
    outs = (out0_ref, out1_ref, out2_ref, out3_ref)
    for head in range(HEADS + 3):
        at = head * HD
        if head == HEADS:
            rows = jnp.broadcast_to(to_column(length_ref[...].astype(F32)), square).astype(BF16)
        else:
            source = at if head < HEADS else at - HD
            part = slice(source, source + HD)
            came_ref, here = (came0_ref, source) if source < CUT else (came1_ref, source - CUT)
            total = keep_ref[:, part] + came_ref[:, here : here + HD] + bias_ref[:, part]
            if head < HEADS + 2:
                half = HD // 2
                swapped = jnp.concatenate([total[:, half:], total[:, :half]], axis=1)
                total = total * cosine + swapped * sine
            rows = total.astype(BF16)
        placed = jnp.dot(placing, rows, preferred_element_type=F32).astype(BF16)
        placed = placed.astype(F32).reshape(HOLDERS, CAP, HD)
        for index, out_ref in enumerate(outs):
            out_ref[:, :, at : at + HD] = placed[2 * index : 2 * index + 2].astype(BF16)


def spread(home, me, keep, came0, came1, bias, cosine, sine, lengths, ids):
    block = jax.ShapeDtypeStruct((2, CAP, ROW_WIDTH), BF16)
    smem = pl.BlockSpec(memory_space=pltpu.SMEM)
    vmem = pl.BlockSpec(memory_space=pltpu.VMEM)
    return pl.pallas_call(
        spread_kernel,
        in_specs=[smem, smem] + [vmem] * 8,
        out_specs=[vmem] * 5,
        out_shape=[block] * 4 + [jax.ShapeDtypeStruct((1, ROWS), jnp.int32)],
        compiler_params=params(8),
        cost_estimate=pl.CostEstimate(
            flops=2 * SLOTS * ROWS * ROW_WIDTH, bytes_accessed=2 * 2**20, transcendentals=0
        ),
    )(home, me, keep, came0, came1, bias, cosine, sine, lengths, ids)


NT = (((1,), (1,)), ((), ()))


def attend_replies(rows_ref, keys_ref, values_ref, out_ref, log_ref, wide_ref):
    wide_ref[...] = rows_ref[:, 0:KEY_AT].astype(F32)
    group = 8
    parts = CAP // group
    lanes = lane_ids((group, HD))
    lines = lax.broadcasted_iota(jnp.int32, (group, HD), 0)
    scores = []
    for part in range(parts):
        slots = slice(part * group, (part + 1) * group)
        stacked = jnp.concatenate(
            [wide_ref[slots, head * HD : (head + 1) * HD] for head in range(HEADS)], axis=0
        ).astype(BF16)
        keys = keys_ref[slots].reshape(group * HD, HD)
        scores.append(lax.dot_general(stacked, keys, NT, preferred_element_type=F32))
    weights = []
    totals = []
    for part in range(parts):
        slots = slice(part * group, (part + 1) * group)
        visible = lanes.astype(F32) < wide_ref[slots, LENGTH_AT : LENGTH_AT + HD]
        visible = jnp.concatenate([visible] * HEADS, axis=0)
        own = jnp.zeros((HEADS * group, HD), F32)
        line = lax.broadcasted_iota(jnp.int32, own.shape, 0) % group
        for slot in range(group):
            own = jnp.where(line == slot, scores[part][:, slot * HD : (slot + 1) * HD], own)
        own = jnp.where(visible, own, MASKED)
        highest = jnp.max(own, axis=1, keepdims=True)
        weight = jnp.exp2((own - highest) * SCALE)
        total = jnp.sum(weight, axis=1, keepdims=True)
        totals.append(total)
        log = jnp.broadcast_to(highest * SCALE + jnp.log2(total), own.shape)
        logs = jnp.zeros((group, HD), F32)
        for head in range(HEADS):
            logs = jnp.where(lanes == head, log[head * group : (head + 1) * group], logs)
        log_ref[slots, :] = logs
        weights.append(
            jnp.concatenate(
                [jnp.where(line == slot, weight, 0.0).astype(BF16) for slot in range(group)], axis=1
            )
        )
    for part in range(parts):
        slots = slice(part * group, (part + 1) * group)
        values = values_ref[slots].reshape(group * HD, HD)
        mixed = jnp.dot(weights[part], values, preferred_element_type=F32) / totals[part]
        for head in range(HEADS):
            out_ref[slots, head * HD : (head + 1) * HD] = mixed[head * group : (head + 1) * group]


def reply_kernel(where_ref, parity_ref, rows_ref, keys_ref, values_ref, out_ref, log_ref, wide_ref):
    attend_replies(
        rows_ref.at[0], keys_ref.at[0], values_ref.at[0], out_ref.at[0], log_ref.at[0], wide_ref
    )


def reply(where, parity, rows, keys, values):
    quarter = 4
    cached = pl.BlockSpec((1, CAP, HD, HD), lambda b, w, q: (2 * b + q[0], 0, 0, 0))
    return pl.pallas_call(
        reply_kernel,
        grid_spec=pltpu.PrefetchScalarGridSpec(
            num_scalar_prefetch=2,
            grid=(quarter,),
            in_specs=[
                pl.BlockSpec((1, CAP, rows.shape[2]), lambda b, w, q: (w[b], 0, 0)),
                cached,
                cached,
            ],
            out_specs=[
                pl.BlockSpec((1, CAP, QW), lambda b, w, q: (b, 0, 0)),
                pl.BlockSpec((1, CAP, HD), lambda b, w, q: (b, 0, 0)),
            ],
            scratch_shapes=[pltpu.VMEM((CAP, KEY_AT), F32)],
        ),
        out_shape=[
            jax.ShapeDtypeStruct((quarter, CAP, QW), F32),
            jax.ShapeDtypeStruct((quarter, CAP, HD), F32),
        ],
        compiler_params=params(12),
        cost_estimate=pl.CostEstimate(
            flops=2 * 10**9, bytes_accessed=8 * 2**20, transcendentals=10**6
        ),
    )(where, parity, rows, keys, values)


def merge_in(out_ref, log_ref, at, other_out, other_log):
    held = log_ref[at]
    highest = jnp.maximum(held, other_log)
    mine = jnp.exp2(held - highest)
    theirs = jnp.exp2(other_log - highest)
    total = mine + theirs
    log_ref[at] = highest + jnp.log2(total)
    mine = mine / total
    theirs = theirs / total
    for head in range(HEADS):
        part = slice(head * HD, (head + 1) * HD)
        out_ref[at, :, part] = (
            out_ref[at, :, part] * mine[:, head : head + 1]
            + other_out(part) * theirs[:, head : head + 1]
        )


def prefix_kernel(own, where_ref, rows_ref, keys_ref, values_ref, *refs):
    if own:
        reply_ref, reply_log_ref, out_ref, log_ref, *scratch = refs
    else:
        parity_ref, cached_keys_ref, cached_values_ref, fresh_ref, sent_ref, *refs = refs
        *scratch, out_ref, log_ref, reply_ref, reply_log_ref, wide_ref = refs
    query_ref, score0_ref, score1_ref, mixed_ref, logs_ref = scratch
    for head in range(HEADS):
        rows = rows_ref[:, :, head * HD : (head + 1) * HD].astype(F32)
        query_ref[head * SLOTS : (head + 1) * SLOTS, :] = rows.reshape(SLOTS, HD).astype(BF16)
    held = (score0_ref, score1_ref)
    total_rows = HEADS * SLOTS

    def score(block):
        queries = query_ref[block * BLOCK : (block + 1) * BLOCK]
        held[block % 2][...] = lax.dot_general(
            queries, keys_ref[...], NT, preferred_element_type=F32
        )

    score(0)
    for block in range(total_rows // BLOCK):
        here = slice(block * BLOCK, (block + 1) * BLOCK)
        scores = held[block % 2][...]
        highest = jnp.max(scores, axis=1, keepdims=True)
        if block + 1 < total_rows // BLOCK:
            score(block + 1)
        if not own and block < reply_ref.shape[0]:
            cached = 2 * block + parity_ref[0]
            attend_replies(
                rows_ref.at[where_ref[block]],
                cached_keys_ref.at[cached],
                cached_values_ref.at[cached],
                reply_ref.at[block],
                reply_log_ref.at[block],
                wide_ref.at[block],
            )
        weights = jnp.exp2((scores - highest) * SCALE)
        total = jnp.sum(weights, axis=1, keepdims=True)
        mixed = jnp.dot(weights.astype(BF16), values_ref[...], preferred_element_type=F32)
        mixed_ref[here] = mixed / total
        logs_ref[here] = jnp.broadcast_to(highest * SCALE + jnp.log2(total), (BLOCK, HD))
    block_lanes = lane_ids((HOLDERS, CAP, HD))
    logs = jnp.zeros((HOLDERS, CAP, HD), F32)
    for head in range(HEADS):
        mine = slice(head * SLOTS, (head + 1) * SLOTS)
        out_ref[:, :, head * HD : (head + 1) * HD] = mixed_ref[mine].reshape(HOLDERS, CAP, HD)
        logs = jnp.where(block_lanes == head, logs_ref[mine].reshape(HOLDERS, CAP, HD), logs)
    log_ref[...] = logs
    for index in range(reply_ref.shape[0]):
        merge_in(
            out_ref,
            log_ref,
            where_ref[index],
            lambda part: reply_ref[index, :, part],
            reply_log_ref[index],
        )
    if own:
        lanes = lane_ids((CAP, HD))
        for block in range(HOLDERS):
            key = rows_ref[block, :, KEY_AT : KEY_AT + HD].astype(F32)
            value = rows_ref[block, :, VALUE_AT : VALUE_AT + HD].astype(F32)
            logs = jnp.zeros((CAP, HD), F32)
            for head in range(HEADS):
                query = rows_ref[block, :, head * HD : (head + 1) * HD].astype(F32)
                score = jnp.sum(query * key, axis=1, keepdims=True) * SCALE
                logs = jnp.where(lanes == head, score, logs)
            merge_in(out_ref, log_ref, block, lambda part: value, logs)
    else:
        log = log_ref[...]
        high = log.astype(BF16).astype(F32)
        middle = (log - high).astype(BF16).astype(F32)
        low = log - high - middle
        packed = jnp.where(block_lanes < HEADS, high, 0.0)
        for index, piece in ((1, middle), (2, low)):
            moved = jnp.concatenate([piece[:, :, HD - 8 * index :], piece[:, :, : HD - 8 * index]], axis=2)
            here = (block_lanes >= 8 * index) & (block_lanes < 8 * index + 8)
            packed = jnp.where(here, moved, packed)
        sent_ref[:, :, 0:QW] = out_ref[...].astype(BF16)
        sent_ref[:, :, QW : QW + HD] = packed.astype(BF16)
        sent_ref[:, :, QW + HD :] = fresh_ref[...]


def prefix(own, where, rows, keys, values, *others):
    smem = pl.BlockSpec(memory_space=pltpu.SMEM)
    vmem = pl.BlockSpec(memory_space=pltpu.VMEM)
    out = (HOLDERS, CAP, QW)
    log = (HOLDERS, CAP, HD)
    scratch = [
        pltpu.VMEM((HEADS * SLOTS, HD), BF16),
        pltpu.VMEM((BLOCK, keys.shape[0]), F32),
        pltpu.VMEM((BLOCK, keys.shape[0]), F32),
        pltpu.VMEM((HEADS * SLOTS, HD), F32),
        pltpu.VMEM((HEADS * SLOTS, HD), F32),
    ]
    if own:
        out_shape = [jax.ShapeDtypeStruct(out, F32), jax.ShapeDtypeStruct(log, F32)]
    else:
        out_shape = [jax.ShapeDtypeStruct((HOLDERS, CAP, ROW_WIDTH), BF16)]
        scratch += [pltpu.VMEM(out, F32), pltpu.VMEM(log, F32)]
        scratch += [pltpu.VMEM((4, CAP, QW), F32), pltpu.VMEM((4, CAP, HD), F32)]
        scratch += [pltpu.VMEM((4, CAP, KEY_AT), F32)]
    work = HEADS * SLOTS * keys.shape[0]
    return pl.pallas_call(
        partial(prefix_kernel, own),
        in_specs=[smem] + [vmem] * 3 + [vmem if own else smem] + [vmem] * (len(others) - 1),
        out_specs=[vmem] * len(out_shape),
        out_shape=out_shape,
        scratch_shapes=scratch,
        compiler_params=params(24),
        cost_estimate=pl.CostEstimate(
            flops=4 * work * HD, bytes_accessed=4 * 2**20, transcendentals=work
        ),
    )(where, rows, keys, values, *others)


def combine_kernel(out_ref, log_ref, came_ref, out0_ref, out1_ref, out2_ref, out3_ref):
    for block in range(HOLDERS):
        packed = came_ref[block, :, QW : QW + HD].astype(F32)
        came_log = packed
        for index in (1, 2):
            came_log = came_log + jnp.concatenate(
                [packed[:, 8 * index :], packed[:, : 8 * index]], axis=1
            )
        held = log_ref[block]
        highest = jnp.maximum(held, came_log)
        mine = jnp.exp2(held - highest)
        theirs = jnp.exp2(came_log - highest)
        total = mine + theirs
        mine = mine / total
        theirs = theirs / total
        target = (out0_ref, out1_ref, out2_ref, out3_ref)[block // 2]
        for head in range(HEADS):
            part = slice(head * HD, (head + 1) * HD)
            target[block % 2, :, part] = (
                out_ref[block, :, part] * mine[:, head : head + 1]
                + came_ref[block, :, part].astype(F32) * theirs[:, head : head + 1]
            ).astype(BF16)


def combine(out, log, came):
    vmem = pl.BlockSpec(memory_space=pltpu.VMEM)
    return pl.pallas_call(
        combine_kernel,
        in_specs=[vmem] * 3,
        out_specs=[vmem] * 4,
        out_shape=[jax.ShapeDtypeStruct((2, CAP, QW), BF16)] * 4,
        compiler_params=params(6),
        cost_estimate=pl.CostEstimate(flops=10**6, bytes_accessed=2 * 2**20, transcendentals=10**5),
    )(out, log, came)


def unplace_kernel(target_ref, near0_ref, near1_ref, near2_ref, near3_ref, far_ref, out_ref, rows_ref):
    for index, near in enumerate((near0_ref, near1_ref, near2_ref, near3_ref)):
        rows_ref[2 * index] = near[0].astype(F32)
        rows_ref[2 * index + 1] = far_ref[index].astype(F32)
    rows = rows_ref[...].reshape(SLOTS, QW).astype(BF16)
    target = target_ref[...]
    placing = jnp.where(
        lax.broadcasted_iota(jnp.int32, (SLOTS, ROWS), 0) == jnp.broadcast_to(target, (SLOTS, ROWS)),
        1.0,
        0.0,
    ).astype(BF16)
    out_ref[...] = lax.dot_general(
        placing, rows, (((0,), (0,)), ((), ())), preferred_element_type=F32
    ).astype(BF16)


def unplace(target, nears, far):
    vmem = pl.BlockSpec(memory_space=pltpu.VMEM)
    return pl.pallas_call(
        unplace_kernel,
        in_specs=[vmem] * 6,
        out_specs=vmem,
        out_shape=jax.ShapeDtypeStruct((ROWS, QW), BF16),
        scratch_shapes=[pltpu.VMEM((HOLDERS, CAP, QW), F32)],
        compiler_params=params(6),
        cost_estimate=pl.CostEstimate(
            flops=2 * SLOTS * ROWS * QW, bytes_accessed=2**20, transcendentals=0
        ),
    )(target, *nears, far)


def store_kernel(me_ref, span_ref, own_ref, other_ref, out_ref):
    for block in range(HOLDERS):
        origin = me_ref[0] ^ block
        for rows_ref, parity in ((own_ref, span_ref[0]), (other_ref, 1 - span_ref[0])):
            for kind in range(2):
                out_ref[kind, 2 * origin + parity] = rows_ref[block, :, kind * HD : (kind + 1) * HD]


def store(me, span, own, other):
    smem = pl.BlockSpec(memory_space=pltpu.SMEM)
    vmem = pl.BlockSpec(memory_space=pltpu.VMEM)
    return pl.pallas_call(
        store_kernel,
        in_specs=[smem, smem, vmem, vmem],
        out_specs=vmem,
        out_shape=jax.ShapeDtypeStruct((2, 2 * HOLDERS, CAP, HD), BF16),
        compiler_params=params(4),
        cost_estimate=pl.CostEstimate(flops=0, bytes_accessed=2**19, transcendentals=0),
    )(me, span, own, other)


def other_pair(values):
    return lax.ppermute(values, "pair", [(0, 1), (1, 0)])


def flip(values, bits):
    return lax.ppermute(values, "memory", [(m, m ^ bits) for m in range(HOLDERS)])


def body(
    hidden,
    norm_gain,
    w_query,
    w_key,
    w_value,
    query_bias,
    key_bias,
    value_bias,
    prefix_keys,
    prefix_values,
    reply_keys,
    reply_values,
    reply_length,
    prefix_ids,
    prompt_home,
):
    me = lax.axis_index("memory").astype(jnp.int32).reshape(1)
    span = lax.axis_index("pair").astype(jnp.int32).reshape(1)

    widened = hidden.astype(F32)
    squares = jnp.sum(widened * widened, axis=1)
    theirs = other_pair(squares)
    keep, send0, send1 = project(
        span,
        squares.reshape(2, ROWS),
        theirs.reshape(2, ROWS),
        hidden,
        norm_gain,
        w_query,
        w_key,
        w_value,
    )
    came0 = other_pair(send0)
    came1 = other_pair(send1)

    half = HD // 2
    ladder = jnp.arange(half, dtype=F32) * (2.0 / HD)
    frequency = jnp.power(ROPE_BASE, -ladder)
    angles = (PREFIX + reply_length).astype(F32)[:, None] * frequency
    cosine = jnp.cos(angles)
    sine = jnp.sin(angles)
    cosine = jnp.concatenate([cosine, cosine], axis=1)
    sine = jnp.concatenate([-sine, sine], axis=1)
    bias = jnp.concatenate([query_bias, key_bias, value_bias]).astype(F32).reshape(1, -1)
    *blocks, target = spread(
        prompt_home, me, keep, came0, came1, bias, cosine, sine, reply_length.reshape(1, ROWS), prefix_ids.reshape(1, ROWS)
    )

    near = {0: blocks[0]}
    for step in (2, 1, 3):
        near[step] = flip(blocks[step], 2 * step)
    near = [near[step] for step in range(4)]
    far = flip(jnp.stack([block[1] for block in near]), 1)
    rows = jnp.stack([piece for step in range(4) for piece in (near[step][0], far[step])])
    partner_rows = other_pair(rows[:, :, :KEY_AT])
    fresh = rows[:, :, KEY_AT:]

    origin = 4 * span[0] + jnp.arange(4, dtype=jnp.int32)
    where = me[0] ^ origin
    caches = (8, CAP, HD, HD)
    keys = reply_keys.reshape(caches)
    values = reply_values.reshape(caches)
    prompt_keys = prefix_keys[0]
    prompt_values = prefix_values[0]
    own_reply = reply(where, span, rows, keys, values)
    own_reply, partner_rows = lax.optimization_barrier((own_reply, partner_rows))
    (sent,) = prefix(
        False,
        where,
        partner_rows,
        prompt_keys,
        prompt_values,
        1 - span,
        keys,
        values,
        fresh,
    )
    came = other_pair(sent)
    rows, sent = lax.optimization_barrier((rows, sent))
    out, log = prefix(True, where, rows, prompt_keys, prompt_values, *own_reply)
    merged = combine(out, log, came)

    nears = {0: merged[0]}
    for step in (2, 1, 3):
        nears[step] = flip(merged[step], 2 * step)
    nears = [nears[step] for step in range(4)]
    fars = flip(jnp.stack([block[1] for block in nears]), 1)
    attention = unplace(target, nears, fars)
    stored = store(me, span, fresh, came[:, :, QW + HD :]).reshape(2, 1, 2 * SLOTS, HD)
    return attention, stored


def solution(mesh):
    in_specs = (
        P("memory", "pair"),
        P("pair"),
        P("pair", "compute"),
        P("pair", "compute"),
        P("pair", "compute"),
        P("compute"),
        P("compute"),
        P("compute"),
        P("memory", "pair", "compute"),
        P("memory", "pair", "compute"),
        P("memory", "pair", None, "compute"),
        P("memory", "pair", None, "compute"),
        P(("memory", "pair")),
        P(("memory", "pair")),
        P(),
    )
    out_specs = (P(("memory", "pair"), "compute"), P(None, "memory", None, "compute"))
    return jax.shard_map(body, mesh=mesh, in_specs=in_specs, out_specs=out_specs, check_vma=False)
```

```python
from functools import partial

import jax
import jax.numpy as jnp
from jax import lax
from jax.experimental import pallas as pl
from jax.experimental.pallas import tpu as pltpu
from jax.sharding import PartitionSpec as P

D = 8192
HD = 128
PREFIX = 8192
EPSILON = 1e-06
ROPE_BASE = 1000000.0
MASKED = -1e30
ROWS = 128
HOLDERS = 8
CAP = 24
HEADS = 8
QW = HEADS * HD
SLOTS = HOLDERS * CAP
BLOCK = 256
PIECES = 8
CUT = QW
LENGTH_AT = QW
KEY_AT = QW + HD
VALUE_AT = QW + 2 * HD
ROW_WIDTH = QW + 3 * HD
SCALE = 1.4426950408889634 / HD**0.5
F32 = jnp.float32
BF16 = jnp.bfloat16


def params(mebibytes):
    return pltpu.CompilerParams(vmem_limit_bytes=mebibytes * 2**20)


def lane_ids(shape):
    return lax.broadcasted_iota(jnp.int32, shape, len(shape) - 1)


def to_column(row):
    size = row.shape[1]
    spread = jnp.broadcast_to(row, (size, size))
    diagonal = lax.broadcasted_iota(jnp.int32, (size, size), 0) == lane_ids((size, size))
    return jnp.sum(jnp.where(diagonal, spread, jnp.zeros_like(spread)), axis=1, keepdims=True)


def normalise(span, mine_ref, theirs_ref, gain_ref, rows_ref, normed_ref):
    inverse = lax.rsqrt((mine_ref[...] + theirs_ref[...]) / D + EPSILON)
    first = to_column(inverse[0:1, :])
    second = to_column(inverse[1:2, :])
    scales = (jnp.where(span == 0, first, second), jnp.where(span == 0, second, first))
    gain = gain_ref[...].astype(F32).reshape(1, -1)
    for where, start in enumerate((span * ROWS, (1 - span) * ROWS)):
        rows = rows_ref[pl.ds(pl.multiple_of(start, ROWS), ROWS), :].astype(F32)
        normed = rows * scales[where] * gain
        normed_ref[where * ROWS : (where + 1) * ROWS, :] = normed.astype(BF16)


def project_queries_kernel(
    span_ref,
    mine_ref,
    theirs_ref,
    hidden_ref,
    gain_ref,
    wq_ref,
    keep_ref,
    send_ref,
    rows_ref,
    query_ref,
    normed_ref,
    sems,
):
    depth = rows_ref.shape[1]
    step = depth // PIECES
    copies = [pltpu.make_async_copy(hidden_ref, rows_ref, sems.at[0])]
    for piece in range(PIECES):
        part = pl.ds(piece * step, step)
        copies.append(
            pltpu.make_async_copy(wq_ref.at[part], query_ref.at[part], sems.at[1 + piece])
        )
    for copy in copies:
        copy.start()
    copies[0].wait()
    normalise(span_ref[0], mine_ref, theirs_ref, gain_ref, rows_ref, normed_ref)
    for piece in range(PIECES):
        copies[1 + piece].wait()
        part = slice(piece * step, (piece + 1) * step)
        for at in range(0, QW, 256):
            here = slice(at, at + 256)
            total = jnp.dot(normed_ref[:, part], query_ref[part, here], preferred_element_type=F32)
            for out_ref, rows in ((keep_ref, total[:ROWS]), (send_ref, total[ROWS:])):
                out_ref[:, here] = rows if piece == 0 else out_ref[:, here] + rows


def project_queries(span, mine, theirs, hidden, gain, w_query):
    depth = hidden.shape[1]
    vmem = pl.BlockSpec(memory_space=pltpu.VMEM)
    hbm = pl.BlockSpec(memory_space=pltpu.HBM)
    return pl.pallas_call(
        project_queries_kernel,
        in_specs=[pl.BlockSpec(memory_space=pltpu.SMEM), vmem, vmem, hbm, vmem, hbm],
        out_specs=[vmem] * 2,
        out_shape=[jax.ShapeDtypeStruct((ROWS, QW), F32)] * 2,
        scratch_shapes=[
            pltpu.VMEM((2 * ROWS, depth), BF16),
            pltpu.VMEM((depth, QW), BF16),
            pltpu.VMEM((2 * ROWS, depth), BF16),
            pltpu.SemaphoreType.DMA((1 + PIECES,)),
        ],
        compiler_params=params(56),
        cost_estimate=pl.CostEstimate(
            flops=2 * 2 * ROWS * depth * QW, bytes_accessed=12 * 2**20, transcendentals=0
        ),
    )(span, mine, theirs, hidden, gain, w_query)


def project_rows_kernel(
    span_ref,
    mine_ref,
    theirs_ref,
    hidden_ref,
    gain_ref,
    wk_ref,
    wv_ref,
    held_ref,
    keep_ref,
    send_ref,
    normed_ref,
):
    normalise(span_ref[0], mine_ref, theirs_ref, gain_ref, hidden_ref, normed_ref)
    keep_ref[:, 0:QW] = held_ref[...]
    for at, w_ref in ((0, wk_ref), (HD, wv_ref)):
        total = jnp.dot(normed_ref[...], w_ref[...], preferred_element_type=F32)
        keep_ref[:, QW + at : QW + at + HD] = total[:ROWS]
        send_ref[:, at : at + HD] = total[ROWS:]


def project_rows(span, mine, theirs, hidden, gain, w_key, w_value, held):
    depth = hidden.shape[1]
    vmem = pl.BlockSpec(memory_space=pltpu.VMEM)
    return pl.pallas_call(
        project_rows_kernel,
        in_specs=[pl.BlockSpec(memory_space=pltpu.SMEM)] + [vmem] * 7,
        out_specs=[vmem] * 2,
        out_shape=[
            jax.ShapeDtypeStruct((ROWS, QW + 2 * HD), F32),
            jax.ShapeDtypeStruct((ROWS, 2 * HD), F32),
        ],
        scratch_shapes=[pltpu.VMEM((2 * ROWS, depth), BF16)],
        compiler_params=params(56),
        cost_estimate=pl.CostEstimate(
            flops=2 * 2 * ROWS * depth * 2 * HD, bytes_accessed=6 * 2**20, transcendentals=0
        ),
    )(span, mine, theirs, hidden, gain, w_key, w_value, held)


def spread_kernel(
    home_ref,
    me_ref,
    keep_ref,
    came0_ref,
    came1_ref,
    bias_ref,
    cos_ref,
    sin_ref,
    length_ref,
    ids_ref,
    out0_ref,
    out1_ref,
    out2_ref,
    out3_ref,
    target_ref,
):
    ids = ids_ref[...]
    owner = jnp.zeros_like(ids)
    for prompt in range(HOLDERS):
        owner = jnp.where(ids == prompt, home_ref[prompt], owner)
    owner_column = to_column(owner.astype(F32))
    square = (ROWS, ROWS)
    earlier = lax.broadcasted_iota(jnp.int32, square, 0) < lane_ids(square)
    same = jnp.broadcast_to(owner_column, square) == jnp.broadcast_to(owner.astype(F32), square)
    rank = jnp.sum(jnp.where(earlier & same, 1.0, 0.0), axis=0, keepdims=True).astype(jnp.int32)
    target = (owner ^ me_ref[0]) * CAP + rank
    target_ref[...] = target
    placing = jnp.where(
        lax.broadcasted_iota(jnp.int32, (SLOTS, ROWS), 0) == jnp.broadcast_to(target, (SLOTS, ROWS)),
        1.0,
        0.0,
    ).astype(BF16)
    cosine = cos_ref[...]
    sine = sin_ref[...]
    outs = (out0_ref, out1_ref, out2_ref, out3_ref)
    for head in range(HEADS + 3):
        at = head * HD
        if head == HEADS:
            rows = jnp.broadcast_to(to_column(length_ref[...].astype(F32)), square).astype(BF16)
        else:
            source = at if head < HEADS else at - HD
            part = slice(source, source + HD)
            came_ref, here = (came0_ref, source) if source < CUT else (came1_ref, source - CUT)
            total = keep_ref[:, part] + came_ref[:, here : here + HD] + bias_ref[:, part]
            if head < HEADS + 2:
                half = HD // 2
                swapped = jnp.concatenate([total[:, half:], total[:, :half]], axis=1)
                total = total * cosine + swapped * sine
            rows = total.astype(BF16)
        placed = jnp.dot(placing, rows, preferred_element_type=F32).astype(BF16)
        placed = placed.astype(F32).reshape(HOLDERS, CAP, HD)
        for index, out_ref in enumerate(outs):
            out_ref[:, :, at : at + HD] = placed[2 * index : 2 * index + 2].astype(BF16)


def spread(home, me, keep, came0, came1, bias, cosine, sine, lengths, ids):
    block = jax.ShapeDtypeStruct((2, CAP, ROW_WIDTH), BF16)
    smem = pl.BlockSpec(memory_space=pltpu.SMEM)
    vmem = pl.BlockSpec(memory_space=pltpu.VMEM)
    return pl.pallas_call(
        spread_kernel,
        in_specs=[smem, smem] + [vmem] * 8,
        out_specs=[vmem] * 5,
        out_shape=[block] * 4 + [jax.ShapeDtypeStruct((1, ROWS), jnp.int32)],
        compiler_params=params(8),
        cost_estimate=pl.CostEstimate(
            flops=2 * SLOTS * ROWS * ROW_WIDTH, bytes_accessed=2 * 2**20, transcendentals=0
        ),
    )(home, me, keep, came0, came1, bias, cosine, sine, lengths, ids)


NT = (((1,), (1,)), ((), ()))


def attend_replies(rows_ref, keys_ref, values_ref, out_ref, log_ref, wide_ref):
    wide_ref[...] = rows_ref[:, 0:KEY_AT].astype(F32)
    group = 8
    parts = CAP // group
    lanes = lane_ids((group, HD))
    lines = lax.broadcasted_iota(jnp.int32, (group, HD), 0)
    scores = []
    for part in range(parts):
        slots = slice(part * group, (part + 1) * group)
        stacked = jnp.concatenate(
            [wide_ref[slots, head * HD : (head + 1) * HD] for head in range(HEADS)], axis=0
        ).astype(BF16)
        keys = keys_ref[slots].reshape(group * HD, HD)
        scores.append(lax.dot_general(stacked, keys, NT, preferred_element_type=F32))
    weights = []
    totals = []
    for part in range(parts):
        slots = slice(part * group, (part + 1) * group)
        visible = lanes.astype(F32) < wide_ref[slots, LENGTH_AT : LENGTH_AT + HD]
        visible = jnp.concatenate([visible] * HEADS, axis=0)
        own = jnp.zeros((HEADS * group, HD), F32)
        line = lax.broadcasted_iota(jnp.int32, own.shape, 0) % group
        for slot in range(group):
            own = jnp.where(line == slot, scores[part][:, slot * HD : (slot + 1) * HD], own)
        own = jnp.where(visible, own, MASKED)
        highest = jnp.max(own, axis=1, keepdims=True)
        weight = jnp.exp2((own - highest) * SCALE)
        total = jnp.sum(weight, axis=1, keepdims=True)
        totals.append(total)
        log = jnp.broadcast_to(highest * SCALE + jnp.log2(total), own.shape)
        logs = jnp.zeros((group, HD), F32)
        for head in range(HEADS):
            logs = jnp.where(lanes == head, log[head * group : (head + 1) * group], logs)
        log_ref[slots, :] = logs
        weights.append(
            jnp.concatenate(
                [jnp.where(line == slot, weight, 0.0).astype(BF16) for slot in range(group)], axis=1
            )
        )
    for part in range(parts):
        slots = slice(part * group, (part + 1) * group)
        values = values_ref[slots].reshape(group * HD, HD)
        mixed = jnp.dot(weights[part], values, preferred_element_type=F32) / totals[part]
        for head in range(HEADS):
            out_ref[slots, head * HD : (head + 1) * HD] = mixed[head * group : (head + 1) * group]


def reply_kernel(where_ref, parity_ref, rows_ref, keys_ref, values_ref, out_ref, log_ref, wide_ref):
    attend_replies(
        rows_ref.at[0], keys_ref.at[0], values_ref.at[0], out_ref.at[0], log_ref.at[0], wide_ref
    )


def reply(where, parity, rows, keys, values):
    quarter = 4
    cached = pl.BlockSpec((1, CAP, HD, HD), lambda b, w, q: (2 * b + q[0], 0, 0, 0))
    return pl.pallas_call(
        reply_kernel,
        grid_spec=pltpu.PrefetchScalarGridSpec(
            num_scalar_prefetch=2,
            grid=(quarter,),
            in_specs=[
                pl.BlockSpec((1, CAP, rows.shape[2]), lambda b, w, q: (w[b], 0, 0)),
                cached,
                cached,
            ],
            out_specs=[
                pl.BlockSpec((1, CAP, QW), lambda b, w, q: (b, 0, 0)),
                pl.BlockSpec((1, CAP, HD), lambda b, w, q: (b, 0, 0)),
            ],
            scratch_shapes=[pltpu.VMEM((CAP, KEY_AT), F32)],
        ),
        out_shape=[
            jax.ShapeDtypeStruct((quarter, CAP, QW), F32),
            jax.ShapeDtypeStruct((quarter, CAP, HD), F32),
        ],
        compiler_params=params(12),
        cost_estimate=pl.CostEstimate(
            flops=2 * 10**9, bytes_accessed=8 * 2**20, transcendentals=10**6
        ),
    )(where, parity, rows, keys, values)


def merge_in(out_ref, log_ref, at, other_out, other_log):
    held = log_ref[at]
    highest = jnp.maximum(held, other_log)
    mine = jnp.exp2(held - highest)
    theirs = jnp.exp2(other_log - highest)
    total = mine + theirs
    log_ref[at] = highest + jnp.log2(total)
    mine = mine / total
    theirs = theirs / total
    for head in range(HEADS):
        part = slice(head * HD, (head + 1) * HD)
        out_ref[at, :, part] = (
            out_ref[at, :, part] * mine[:, head : head + 1]
            + other_out(part) * theirs[:, head : head + 1]
        )


def prefix_kernel(own, where_ref, rows_ref, keys_ref, values_ref, *refs):
    if own:
        reply_ref, reply_log_ref, out_ref, log_ref, *scratch = refs
    else:
        parity_ref, cached_keys_ref, cached_values_ref, fresh_ref, sent_ref, *refs = refs
        *scratch, out_ref, log_ref, reply_ref, reply_log_ref, wide_ref = refs
    query_ref, score0_ref, score1_ref, mixed_ref, logs_ref = scratch
    for head in range(HEADS):
        rows = rows_ref[:, :, head * HD : (head + 1) * HD].astype(F32)
        query_ref[head * SLOTS : (head + 1) * SLOTS, :] = rows.reshape(SLOTS, HD).astype(BF16)
    held = (score0_ref, score1_ref)
    total_rows = HEADS * SLOTS

    def score(block):
        queries = query_ref[block * BLOCK : (block + 1) * BLOCK]
        held[block % 2][...] = lax.dot_general(
            queries, keys_ref[...], NT, preferred_element_type=F32
        )

    score(0)
    for block in range(total_rows // BLOCK):
        here = slice(block * BLOCK, (block + 1) * BLOCK)
        scores = held[block % 2][...]
        highest = jnp.max(scores, axis=1, keepdims=True)
        if block + 1 < total_rows // BLOCK:
            score(block + 1)
        if not own and block < reply_ref.shape[0]:
            cached = 2 * block + parity_ref[0]
            attend_replies(
                rows_ref.at[where_ref[block]],
                cached_keys_ref.at[cached],
                cached_values_ref.at[cached],
                reply_ref.at[block],
                reply_log_ref.at[block],
                wide_ref.at[block],
            )
        weights = jnp.exp2((scores - highest) * SCALE)
        total = jnp.sum(weights, axis=1, keepdims=True)
        mixed = jnp.dot(weights.astype(BF16), values_ref[...], preferred_element_type=F32)
        mixed_ref[here] = mixed / total
        logs_ref[here] = jnp.broadcast_to(highest * SCALE + jnp.log2(total), (BLOCK, HD))
    block_lanes = lane_ids((HOLDERS, CAP, HD))
    logs = jnp.zeros((HOLDERS, CAP, HD), F32)
    for head in range(HEADS):
        mine = slice(head * SLOTS, (head + 1) * SLOTS)
        out_ref[:, :, head * HD : (head + 1) * HD] = mixed_ref[mine].reshape(HOLDERS, CAP, HD)
        logs = jnp.where(block_lanes == head, logs_ref[mine].reshape(HOLDERS, CAP, HD), logs)
    log_ref[...] = logs
    for index in range(reply_ref.shape[0]):
        merge_in(
            out_ref,
            log_ref,
            where_ref[index],
            lambda part: reply_ref[index, :, part],
            reply_log_ref[index],
        )
    if own:
        lanes = lane_ids((CAP, HD))
        for block in range(HOLDERS):
            key = rows_ref[block, :, KEY_AT : KEY_AT + HD].astype(F32)
            value = rows_ref[block, :, VALUE_AT : VALUE_AT + HD].astype(F32)
            logs = jnp.zeros((CAP, HD), F32)
            for head in range(HEADS):
                query = rows_ref[block, :, head * HD : (head + 1) * HD].astype(F32)
                score = jnp.sum(query * key, axis=1, keepdims=True) * SCALE
                logs = jnp.where(lanes == head, score, logs)
            merge_in(out_ref, log_ref, block, lambda part: value, logs)
    else:
        log = log_ref[...]
        high = log.astype(BF16).astype(F32)
        middle = (log - high).astype(BF16).astype(F32)
        low = log - high - middle
        packed = jnp.where(block_lanes < HEADS, high, 0.0)
        for index, piece in ((1, middle), (2, low)):
            moved = jnp.concatenate([piece[:, :, HD - 8 * index :], piece[:, :, : HD - 8 * index]], axis=2)
            here = (block_lanes >= 8 * index) & (block_lanes < 8 * index + 8)
            packed = jnp.where(here, moved, packed)
        sent_ref[:, :, 0:QW] = out_ref[...].astype(BF16)
        sent_ref[:, :, QW : QW + HD] = packed.astype(BF16)
        sent_ref[:, :, QW + HD :] = fresh_ref[...]


def prefix(own, where, rows, keys, values, *others):
    smem = pl.BlockSpec(memory_space=pltpu.SMEM)
    vmem = pl.BlockSpec(memory_space=pltpu.VMEM)
    out = (HOLDERS, CAP, QW)
    log = (HOLDERS, CAP, HD)
    scratch = [
        pltpu.VMEM((HEADS * SLOTS, HD), BF16),
        pltpu.VMEM((BLOCK, keys.shape[0]), F32),
        pltpu.VMEM((BLOCK, keys.shape[0]), F32),
        pltpu.VMEM((HEADS * SLOTS, HD), F32),
        pltpu.VMEM((HEADS * SLOTS, HD), F32),
    ]
    if own:
        out_shape = [jax.ShapeDtypeStruct(out, F32), jax.ShapeDtypeStruct(log, F32)]
    else:
        out_shape = [jax.ShapeDtypeStruct((HOLDERS, CAP, ROW_WIDTH), BF16)]
        scratch += [pltpu.VMEM(out, F32), pltpu.VMEM(log, F32)]
        scratch += [pltpu.VMEM((4, CAP, QW), F32), pltpu.VMEM((4, CAP, HD), F32)]
        scratch += [pltpu.VMEM((4, CAP, KEY_AT), F32)]
    work = HEADS * SLOTS * keys.shape[0]
    return pl.pallas_call(
        partial(prefix_kernel, own),
        in_specs=[smem] + [vmem] * 3 + [vmem if own else smem] + [vmem] * (len(others) - 1),
        out_specs=[vmem] * len(out_shape),
        out_shape=out_shape,
        scratch_shapes=scratch,
        compiler_params=params(24),
        cost_estimate=pl.CostEstimate(
            flops=4 * work * HD, bytes_accessed=4 * 2**20, transcendentals=work
        ),
    )(where, rows, keys, values, *others)


def combine_kernel(out_ref, log_ref, came_ref, out0_ref, out1_ref, out2_ref, out3_ref):
    for block in range(HOLDERS):
        packed = came_ref[block, :, QW : QW + HD].astype(F32)
        came_log = packed
        for index in (1, 2):
            came_log = came_log + jnp.concatenate(
                [packed[:, 8 * index :], packed[:, : 8 * index]], axis=1
            )
        held = log_ref[block]
        highest = jnp.maximum(held, came_log)
        mine = jnp.exp2(held - highest)
        theirs = jnp.exp2(came_log - highest)
        total = mine + theirs
        mine = mine / total
        theirs = theirs / total
        target = (out0_ref, out1_ref, out2_ref, out3_ref)[block // 2]
        for head in range(HEADS):
            part = slice(head * HD, (head + 1) * HD)
            target[block % 2, :, part] = (
                out_ref[block, :, part] * mine[:, head : head + 1]
                + came_ref[block, :, part].astype(F32) * theirs[:, head : head + 1]
            ).astype(BF16)


def combine(out, log, came):
    vmem = pl.BlockSpec(memory_space=pltpu.VMEM)
    return pl.pallas_call(
        combine_kernel,
        in_specs=[vmem] * 3,
        out_specs=[vmem] * 4,
        out_shape=[jax.ShapeDtypeStruct((2, CAP, QW), BF16)] * 4,
        compiler_params=params(6),
        cost_estimate=pl.CostEstimate(flops=10**6, bytes_accessed=2 * 2**20, transcendentals=10**5),
    )(out, log, came)


def unplace_kernel(target_ref, near0_ref, near1_ref, near2_ref, near3_ref, far_ref, out_ref, rows_ref):
    for index, near in enumerate((near0_ref, near1_ref, near2_ref, near3_ref)):
        rows_ref[2 * index] = near[0].astype(F32)
        rows_ref[2 * index + 1] = far_ref[index].astype(F32)
    rows = rows_ref[...].reshape(SLOTS, QW).astype(BF16)
    target = target_ref[...]
    placing = jnp.where(
        lax.broadcasted_iota(jnp.int32, (SLOTS, ROWS), 0) == jnp.broadcast_to(target, (SLOTS, ROWS)),
        1.0,
        0.0,
    ).astype(BF16)
    out_ref[...] = lax.dot_general(
        placing, rows, (((0,), (0,)), ((), ())), preferred_element_type=F32
    ).astype(BF16)


def unplace(target, nears, far):
    vmem = pl.BlockSpec(memory_space=pltpu.VMEM)
    return pl.pallas_call(
        unplace_kernel,
        in_specs=[vmem] * 6,
        out_specs=vmem,
        out_shape=jax.ShapeDtypeStruct((ROWS, QW), BF16),
        scratch_shapes=[pltpu.VMEM((HOLDERS, CAP, QW), F32)],
        compiler_params=params(6),
        cost_estimate=pl.CostEstimate(
            flops=2 * SLOTS * ROWS * QW, bytes_accessed=2**20, transcendentals=0
        ),
    )(target, *nears, far)


def store_kernel(me_ref, span_ref, own_ref, other_ref, out_ref):
    for block in range(HOLDERS):
        origin = me_ref[0] ^ block
        for rows_ref, parity in ((own_ref, span_ref[0]), (other_ref, 1 - span_ref[0])):
            for kind in range(2):
                out_ref[kind, 2 * origin + parity] = rows_ref[block, :, kind * HD : (kind + 1) * HD]


def store(me, span, own, other):
    smem = pl.BlockSpec(memory_space=pltpu.SMEM)
    vmem = pl.BlockSpec(memory_space=pltpu.VMEM)
    return pl.pallas_call(
        store_kernel,
        in_specs=[smem, smem, vmem, vmem],
        out_specs=vmem,
        out_shape=jax.ShapeDtypeStruct((2, 2 * HOLDERS, CAP, HD), BF16),
        compiler_params=params(4),
        cost_estimate=pl.CostEstimate(flops=0, bytes_accessed=2**19, transcendentals=0),
    )(me, span, own, other)


def other_pair(values):
    return lax.ppermute(values, "pair", [(0, 1), (1, 0)])


def flip(values, bits):
    return lax.ppermute(values, "memory", [(m, m ^ bits) for m in range(HOLDERS)])


def body(
    hidden,
    norm_gain,
    w_query,
    w_key,
    w_value,
    query_bias,
    key_bias,
    value_bias,
    prefix_keys,
    prefix_values,
    reply_keys,
    reply_values,
    reply_length,
    prefix_ids,
    prompt_home,
):
    me = lax.axis_index("memory").astype(jnp.int32).reshape(1)
    span = lax.axis_index("pair").astype(jnp.int32).reshape(1)

    widened = hidden.astype(F32)
    squares = jnp.sum(widened * widened, axis=1)
    theirs = other_pair(squares)
    sums = (squares.reshape(2, ROWS), theirs.reshape(2, ROWS))
    held, send0 = project_queries(span, *sums, hidden, norm_gain, w_query)
    came0 = other_pair(send0)
    keep, send1 = project_rows(span, *sums, hidden, norm_gain, w_key, w_value, held)
    came1 = other_pair(send1)

    half = HD // 2
    ladder = jnp.arange(half, dtype=F32) * (2.0 / HD)
    frequency = jnp.power(ROPE_BASE, -ladder)
    angles = (PREFIX + reply_length).astype(F32)[:, None] * frequency
    cosine = jnp.cos(angles)
    sine = jnp.sin(angles)
    cosine = jnp.concatenate([cosine, cosine], axis=1)
    sine = jnp.concatenate([-sine, sine], axis=1)
    bias = jnp.concatenate([query_bias, key_bias, value_bias]).astype(F32).reshape(1, -1)
    *blocks, target = spread(
        prompt_home, me, keep, came0, came1, bias, cosine, sine, reply_length.reshape(1, ROWS), prefix_ids.reshape(1, ROWS)
    )

    near = {0: blocks[0]}
    for step in (2, 1, 3):
        near[step] = flip(blocks[step], 2 * step)
    near = [near[step] for step in range(4)]
    far = flip(jnp.stack([block[1] for block in near]), 1)
    rows = jnp.stack([piece for step in range(4) for piece in (near[step][0], far[step])])
    partner_rows = other_pair(rows[:, :, :KEY_AT])
    fresh = rows[:, :, KEY_AT:]

    origin = 4 * span[0] + jnp.arange(4, dtype=jnp.int32)
    where = me[0] ^ origin
    caches = (8, CAP, HD, HD)
    keys = reply_keys.reshape(caches)
    values = reply_values.reshape(caches)
    prompt_keys = prefix_keys[0]
    prompt_values = prefix_values[0]
    own_reply = reply(where, span, rows, keys, values)
    own_reply, partner_rows = lax.optimization_barrier((own_reply, partner_rows))
    (sent,) = prefix(
        False,
        where,
        partner_rows,
        prompt_keys,
        prompt_values,
        1 - span,
        keys,
        values,
        fresh,
    )
    came = other_pair(sent)
    rows, sent = lax.optimization_barrier((rows, sent))
    out, log = prefix(True, where, rows, prompt_keys, prompt_values, *own_reply)
    merged = combine(out, log, came)

    nears = {0: merged[0]}
    for step in (2, 1, 3):
        nears[step] = flip(merged[step], 2 * step)
    nears = [nears[step] for step in range(4)]
    fars = flip(jnp.stack([block[1] for block in nears]), 1)
    attention = unplace(target, nears, fars)
    stored = store(me, span, fresh, came[:, :, QW + HD :]).reshape(2, 1, 2 * SLOTS, HD)
    return attention, stored


def solution(mesh):
    in_specs = (
        P("memory", "pair"),
        P("pair"),
        P("pair", "compute"),
        P("pair", "compute"),
        P("pair", "compute"),
        P("compute"),
        P("compute"),
        P("compute"),
        P("memory", "pair", "compute"),
        P("memory", "pair", "compute"),
        P("memory", "pair", None, "compute"),
        P("memory", "pair", None, "compute"),
        P(("memory", "pair")),
        P(("memory", "pair")),
        P(),
    )
    out_specs = (P(("memory", "pair"), "compute"), P(None, "memory", None, "compute"))
    return jax.shard_map(body, mesh=mesh, in_specs=in_specs, out_specs=out_specs, check_vma=False)
```
